256 devices in a mesh: lat: 8 (over y_lo, x), lon: 32 (over y_hi, z, core).
Axes of the slice: x: 4, y: 4 (y_hi: 2, y_lo: 2; y = y_hi * 2 + y_lo), z: 8, core: 2. Of those that a mesh axis runs over, the one named last changes fastest.
Arguments:
- queries: bfloat16 [64, 1024, 512], P('lat', 'lon'), may hold values from -8 to 8
- keys: bfloat16 [64, 1024, 512], P('lat', 'lon'), may hold values from -8 to 8
- values: bfloat16 [64, 1024, 512], P('lat', 'lon'), may hold values from -6 to 6
- grad_out: bfloat16 [64, 1024, 512], P('lat', 'lon'), may hold values from -6 to 6
- sink_logits: float32 [8], replicated, may hold values from 4 to 8
Outputs:
- attended: bfloat16 [64, 1024, 512], P('lat', 'lon')
- query_grad: bfloat16 [64, 1024, 512], P('lat', 'lon')
- key_grad: bfloat16 [64, 1024, 512], P('lat', 'lon')
- value_grad: bfloat16 [64, 1024, 512], P('lat', 'lon')
- sink_grad: float32 [8], replicated
The draws below stay inside these ranges and needn't reach their ends.
All inputs are finite; a program needn't handle non-finite values.
Results may differ from the reference program's by a relative error of at most 0.0085.
Values may be sent and summed in bfloat16 or wider, within the bound.
A program may use at most 64 MiB of HBM per device.

```python
import jax
import jax.numpy as jnp
from jax import lax

HEADS = 8
HEAD_DIM = 64
D = 512
WIN = 13
CLAT = 8
NLAT = 64
NLON = 1024
N_LAT = 8


def block_levels(key, extent, split, smallest, high):
    level, own = 1.0, jax.random.fold_in(key, 6)
    for axis_at, parts in split:
        steps = jnp.exp(jax.random.uniform(jax.random.fold_in(own, axis_at), (parts,), jnp.float32, smallest / len(split), high / len(split)))
        level = level * jnp.repeat(steps, extent[axis_at] // parts).reshape([-1 if axis == axis_at else 1 for axis in range(len(extent))])
    return level


def noise(stream_key, shape, spread, most, pieces=(), held_as=jnp.bfloat16):
    result = spread * jax.random.normal(stream_key, shape, jnp.float32)
    if pieces:
        result = result * block_levels(stream_key, shape, pieces, -0.22, 0.18)
    return jnp.clip(result, -most, most).astype(held_as)


def setup_inputs(seed: int = 0) -> dict:
    arg_keys = jax.random.split(jax.random.key(seed), 6)
    queries = noise(arg_keys[0], (NLAT, NLON, D), 1.6, 8.0, ((0, 8), (1, 32)))
    keys = noise(arg_keys[1], (NLAT, NLON, D), 1.6, 8.0, ((0, 8), (1, 32)))
    values = noise(arg_keys[2], (NLAT, NLON, D), 1.0, 6.0, ((0, 8), (1, 32)))
    grad_out = noise(arg_keys[3], (NLAT, NLON, D), 1.0, 6.0, ((0, 8), (1, 32)))
    sink_logits = jnp.clip(jax.random.uniform(arg_keys[4], (HEADS,), jnp.float32, 4.0, 8.0), 4.0, 8.0)
    return dict(queries=queries, keys=keys, values=values, grad_out=grad_out, sink_logits=sink_logits)


softcap = 8.0

def widen(field, radius):
    wrapped = jnp.concatenate([field[:, -radius:], field, field[:, :radius]], axis=1)
    widths = [(radius, radius)] + [(0, 0)] * (field.ndim - 1)
    return jnp.pad(wrapped, widths)

def split_heads(piece):
    return piece.astype(jnp.float32).reshape(piece.shape[0], piece.shape[1], HEADS, HEAD_DIM)

def reference(queries, keys, values, grad_out, sink_logits):
    radius = WIN // 2
    score_scale = HEAD_DIM ** (-0.5)
    sink_weight = jnp.exp(sink_logits - softcap)
    keys_wide = widen(keys, radius)
    values_wide = widen(values, radius)
    offsets = jnp.arange(WIN * WIN, dtype=jnp.int32)
    band_ids = jnp.arange(N_LAT, dtype=jnp.int32)

    def view(field, band_start, offset):
        shift_row = (offset // WIN).astype(jnp.int32)
        shift_col = (offset % WIN).astype(jnp.int32)
        return lax.dynamic_slice(field, (band_start + shift_row, shift_col, jnp.int32(0)), (CLAT, NLON, field.shape[2]))

    def row_valid(band_start, offset):
        rows = band_start + offset // WIN - radius + jnp.arange(CLAT, dtype=jnp.int32)
        return ((rows >= 0) & (rows < NLAT))[:, None, None]

    def forward_band(band_index):
        band_start = (band_index * CLAT).astype(jnp.int32)
        query_band = split_heads(lax.dynamic_slice_in_dim(queries, band_start, CLAT, 0))
        grad_band = split_heads(lax.dynamic_slice_in_dim(grad_out, band_start, CLAT, 0))

        def scores(offset):
            key_piece = split_heads(view(keys_wide, band_start, offset))
            raw_scores = lax.optimization_barrier(jnp.sum(query_band * key_piece, axis=-1)) * score_scale
            squashed = jnp.tanh(raw_scores / softcap)
            weights = jnp.where(row_valid(band_start, offset), jnp.exp(softcap * squashed - softcap), 0.0)
            return (squashed, weights, key_piece)

        def add_weights(running, offset):
            return (running + scores(offset)[1], None)
        start_sum = jnp.zeros((CLAT, NLON, HEADS), jnp.float32) + sink_weight
        denominator, unused = lax.scan(add_weights, start_sum, offsets)

        def add_output(running, offset):
            out_sum, delta_sum = running
            squashed, weights, key_piece = scores(offset)
            attention = weights / denominator
            attention_low = lax.optimization_barrier(attention.astype(jnp.bfloat16)).astype(jnp.float32)
            value_piece = split_heads(view(values_wide, band_start, offset))
            out_sum = out_sum + attention_low[..., None] * value_piece
            prob_grad = lax.optimization_barrier(jnp.sum(grad_band * value_piece, axis=-1))
            return ((out_sum, delta_sum + attention * prob_grad), None)
        zeros_full = jnp.zeros((CLAT, NLON, HEADS, HEAD_DIM), jnp.float32)
        zeros_head = jnp.zeros((CLAT, NLON, HEADS), jnp.float32)
        (out_sum, delta_sum), unused = lax.scan(add_output, (zeros_full, zeros_head), offsets)

        def add_query_grad(running, offset):
            squashed, weights, key_piece = scores(offset)
            attention = weights / denominator
            value_piece = split_heads(view(values_wide, band_start, offset))
            prob_grad = lax.optimization_barrier(jnp.sum(grad_band * value_piece, axis=-1))
            score_grad = attention * (prob_grad - delta_sum) * (1.0 - squashed * squashed) * score_scale
            score_grad = lax.optimization_barrier(score_grad.astype(jnp.bfloat16)).astype(jnp.float32)
            return (running + score_grad[..., None] * key_piece, None)
        query_sum, unused = lax.scan(add_query_grad, zeros_full, offsets)
        sink_part = -lax.optimization_barrier(jnp.sum(sink_weight / denominator * delta_sum, axis=(0, 1)))
        return (out_sum.reshape(CLAT, NLON, D).astype(jnp.bfloat16), query_sum.reshape(CLAT, NLON, D).astype(jnp.bfloat16), denominator, delta_sum, sink_part)
    attended, query_grad, denominator, delta_sum, sink_parts = lax.map(forward_band, band_ids)
    attended = attended.reshape(NLAT, NLON, D)
    query_grad = query_grad.reshape(NLAT, NLON, D)
    denominator = denominator.reshape(NLAT, NLON, HEADS)
    delta_sum = delta_sum.reshape(NLAT, NLON, HEADS)
    sink_grad = lax.optimization_barrier(jnp.sum(sink_parts, axis=0))
    queries_wide = widen(queries, radius)
    grad_wide = widen(grad_out, radius)
    denom_wide = widen(denominator - 1.0, radius) + 1.0
    delta_wide = widen(delta_sum, radius)

    def backward_band(band_index):
        band_start = (band_index * CLAT).astype(jnp.int32)
        key_band = split_heads(lax.dynamic_slice_in_dim(keys, band_start, CLAT, 0))
        value_band = split_heads(lax.dynamic_slice_in_dim(values, band_start, CLAT, 0))

        def add_key_grad(running, offset):
            key_sum, value_sum = running
            query_piece = split_heads(view(queries_wide, band_start, offset))
            grad_piece = split_heads(view(grad_wide, band_start, offset))
            raw_scores = lax.optimization_barrier(jnp.sum(query_piece * key_band, axis=-1)) * score_scale
            squashed = jnp.tanh(raw_scores / softcap)
            weights = jnp.where(row_valid(band_start, offset), jnp.exp(softcap * squashed - softcap), 0.0)
            attention = weights / view(denom_wide, band_start, offset)
            attention_low = lax.optimization_barrier(attention.astype(jnp.bfloat16)).astype(jnp.float32)
            prob_grad = lax.optimization_barrier(jnp.sum(grad_piece * value_band, axis=-1))
            score_grad = attention * (prob_grad - view(delta_wide, band_start, offset)) * (1.0 - squashed * squashed) * score_scale
            score_grad = lax.optimization_barrier(score_grad.astype(jnp.bfloat16)).astype(jnp.float32)
            key_sum = key_sum + score_grad[..., None] * query_piece
            value_sum = value_sum + attention_low[..., None] * grad_piece
            return ((key_sum, value_sum), None)
        zeros_full = jnp.zeros((CLAT, NLON, HEADS, HEAD_DIM), jnp.float32)
        (key_sum, value_sum), unused = lax.scan(add_key_grad, (zeros_full, zeros_full), offsets)
        return (key_sum.reshape(CLAT, NLON, D).astype(jnp.bfloat16), value_sum.reshape(CLAT, NLON, D).astype(jnp.bfloat16))
    key_grad, value_grad = lax.map(backward_band, band_ids)
    key_grad = key_grad.reshape(NLAT, NLON, D)
    value_grad = value_grad.reshape(NLAT, NLON, D)
    return (attended, query_grad, key_grad, value_grad, sink_grad)
```

```python
import functools
import math

import jax
import jax.numpy as jnp
from jax import lax
from jax.experimental import pallas as pl
from jax.experimental.pallas import tpu as pltpu
from jax.sharding import PartitionSpec as P

WIN = 13
RADIUS = WIN // 2
SOFTCAP = 8.0
PAIRS = 4
ROWS = 8
COLS = 32
WIDE = 8
EXT_ROWS = ROWS + 2 * RADIUS
EXT_COLS = COLS + 2 * WIDE
TILE = 16
SPAN = TILE + 2 * WIDE
CHUNK = 4
N_CHUNK = EXT_ROWS // CHUNK
KEYS = CHUNK * SPAN
QN = ROWS * TILE
LANES = 128
N_LAT = 8
N_LON = 32
N_Z = 8
MESH = pl.DeviceIdType.MESH
BF16 = jnp.bfloat16
F32 = jnp.float32
EXP2_RATE = SOFTCAP * math.log2(math.e)

NT = (((1,), (1,)), ((), ()))
TN = (((0,), (0,)), ((), ()))


def dot(a, b, dims=(((1,), (0,)), ((), ()))):
    return lax.dot_general(a, b, dims, preferred_element_type=F32)


def head_blocks(turned):
    first = lax.broadcasted_iota(jnp.int32, (LANES, QN), 0) < LANES // 2
    return jnp.concatenate(
        [jnp.where(first, turned, 0.0), jnp.where(first, 0.0, turned)], axis=1
    )


def own_heads(both):
    first = lax.broadcasted_iota(jnp.int32, (LANES, QN), 0) < LANES // 2
    return jnp.where(first, both[:, :QN], both[:, QN:])


def kernel(
    q_hbm, k_hbm, v_hbm, g_hbm, sink_ref,
    o_hbm, dq_hbm, dk_hbm, dv_hbm, sg_ref,
    q_s, kv_s, g_s, ext, top, bot, mask,
    strip_to, strip_from, gstrip_to, gstrip_from, rim_to, rim_from,
    acc, e_s, u_s, out_s, sk, sk_all,
    in_sem, out_sem, lat_send, lat_recv, strip_send, strip_recv,
    gs_send, gs_recv, rim_send, rim_recv, sk_send, sk_recv, entered, met,
):
    a = lax.axis_index("lat")
    b = lax.axis_index("lon")
    up = (lax.rem(a + N_LAT - 1, N_LAT), b)
    down = (lax.rem(a + 1, N_LAT), b)
    left = (a, lax.rem(b + N_LON - 1, N_LON))
    right = (a, lax.rem(b + 1, N_LON))
    sides = (left, right)
    column = lax.rem(b, 2 * N_Z)
    z = column // 2
    is_first = column == 0
    is_last = column == 2 * N_Z - 1

    def lat_peer(d):
        return (lax.rem(a + d, N_LAT), b)

    def quad_peer(d):
        other = lax.rem(lax.rem(b, 2) + 2 * (b // (2 * N_Z)) + d, 4)
        return (a, lax.rem(other, 2) + 2 * z + 2 * N_Z * (other // 2))

    def z_peer(d):
        return (a, lax.rem(b, 2) + 2 * lax.rem(z + d, N_Z) + 2 * N_Z * (b // (2 * N_Z)))

    def load(i, p):
        src = (q_hbm, k_hbm, v_hbm, g_hbm)[i]
        dst = (q_s, kv_s.at[0], kv_s.at[1], g_s)[i]
        return pltpu.make_async_copy(
            src.at[:, :, pl.ds(pl.multiple_of(p * LANES, LANES), LANES)], dst.at[p], in_sem.at[i, p]
        )

    for p in range(PAIRS):
        for i in (1, 2):
            load(i, p).start()
    for p in range(PAIRS):
        for i in (0, 3):
            load(i, p).start()

    barrier = pltpu.get_barrier_semaphore()

    def greet(device):
        pl.semaphore_signal(barrier, inc=1, device_id=device, device_id_type=MESH)

    for d in range(1, N_LAT):
        greet(lat_peer(d))
    for d in range(1, 4):
        greet(quad_peer(d))
    @pl.when(jnp.logical_not(is_last))
    def _():
        greet(right)

    @pl.when(is_first)
    def _():
        greet(left)

    for d in range(1, N_Z):
        @pl.when(z + d < N_Z)
        def _():
            greet(z_peer(d))

    expect = N_LAT - 1 + 3 + z + jnp.where(is_first, 0, 1) + jnp.where(is_last, 1, 0)
    pl.semaphore_wait(barrier, expect)

    def lat_copy(p, i, side):
        src = (k_hbm, v_hbm)[i]
        first_row = (0, ROWS - RADIUS)[side]
        return pltpu.make_async_remote_copy(
            src_ref=src.at[
                first_row : first_row + RADIUS, :, pl.ds(pl.multiple_of(p * LANES, LANES), LANES)
            ],
            dst_ref=(bot, top)[side].at[p, i],
            send_sem=lat_send.at[p, i, side],
            recv_sem=lat_recv.at[p, i, side],
            device_id=(up, down)[side],
            device_id_type=MESH,
        )

    for p in range(PAIRS):
        for i in range(2):
            for side in range(2):
                lat_copy(p, i, side).start()

    @pl.when(jnp.logical_not(is_first))
    def _():
        pl.semaphore_signal(entered.at[1], inc=1, device_id=left, device_id_type=MESH)

    @pl.when(is_last)
    def _():
        pl.semaphore_signal(entered.at[0], inc=1, device_id=right, device_id_type=MESH)

    for d in range(1, N_Z):
        @pl.when(z - d >= 0)
        def _():
            pl.semaphore_signal(met, inc=1, device_id=z_peer(N_Z - d), device_id_type=MESH)

    key = lax.broadcasted_iota(jnp.int32, (EXT_ROWS * SPAN, QN), 0)
    query = lax.broadcasted_iota(jnp.int32, (EXT_ROWS * SPAN, QN), 1)
    key_row = key // SPAN - RADIUS
    row_gap = key_row - query // TILE
    col_gap = lax.rem(key, SPAN) - WIDE - lax.rem(query, TILE)
    whole_row = a * ROWS + key_row
    meets = (
        (row_gap >= -RADIUS) & (row_gap <= RADIUS) & (col_gap >= -RADIUS) & (col_gap <= RADIUS)
        & (whole_row >= 0) & (whole_row < N_LAT * ROWS)
    )
    mask[...] = jnp.where(meets, 1.0, 0.0)

    def rows_of(p, i, r):
        if r < RADIUS:
            return top[p, i, r].astype(F32)
        if r < RADIUS + ROWS:
            return kv_s[i, p, r - RADIUS].astype(F32)
        return bot[p, i, r - RADIUS - ROWS].astype(F32)

    def pack(p, first, last):
        for rp in range(first, last):
            for i in range(2):
                upper, lower = rows_of(p, i, 2 * rp), rows_of(p, i, 2 * rp + 1)
                strip_to[p, 0, rp, i] = jnp.concatenate([upper[:WIDE], lower[:WIDE]], 0).astype(BF16)
                strip_to[p, 1, rp, i] = jnp.concatenate(
                    [upper[COLS - WIDE :], lower[COLS - WIDE :]], 0
                ).astype(BF16)

    spans = ((3, 4), (0, 3), (7, 3))

    def strip_copy(p, side, part):
        first, count = spans[part]
        return pltpu.make_async_remote_copy(
            src_ref=strip_to.at[p, side, first : first + count],
            dst_ref=strip_from.at[p, 1 - side, first : first + count],
            send_sem=strip_send.at[p, side, part],
            recv_sem=strip_recv.at[p, 1 - side, part],
            device_id=sides[side],
            device_id_type=MESH,
        )

    for p in range(PAIRS):
        for i in (1, 2):
            load(i, p).wait()
        pack(p, 3, 7)

    @pl.when(jnp.logical_not(is_last))
    def _():
        pl.semaphore_wait(entered.at[1], 1)

    @pl.when(is_first)
    def _():
        pl.semaphore_wait(entered.at[0], 1)

    for p in range(PAIRS):
        for side in range(2):
            strip_copy(p, side, 0).start()

    acc[...] = jnp.zeros_like(acc)

    def stage_a(p):
        for i in range(2):
            for side in range(2):
                lat_copy(p, i, side).wait_recv()
        pack(p, 0, 3)
        pack(p, 7, 10)
        for side in range(2):
            for part in (1, 2):
                strip_copy(p, side, part).start()

    def stage_ext(p):
        for side in range(2):
            for part in range(3):
                strip_copy(p, side, part).wait_recv()
        for rp in range(EXT_ROWS // 2):
            for i in range(2):
                west = strip_from[p, 0, rp, i].astype(F32)
                east = strip_from[p, 1, rp, i].astype(F32)
                for j in range(2):
                    half = slice(j * WIDE, (j + 1) * WIDE)
                    ext[i, 2 * rp + j] = jnp.concatenate(
                        [west[half], rows_of(p, i, 2 * rp + j), east[half]], 0
                    ).astype(BF16)

    def attend(p, tile):
        at = pl.multiple_of(tile * TILE, TILE)
        cols = pl.ds(at, TILE)
        span = pl.ds(at, SPAN)
        q_turned = q_s[p, :, cols, :].reshape(QN, LANES).astype(F32).T
        g_turned = g_s[p, :, cols, :].reshape(QN, LANES).astype(F32).T
        q_blocks = head_blocks(q_turned)
        g_blocks = head_blocks(g_turned)
        q_low = (q_blocks * (1.0 / 64.0)).astype(BF16)
        g_low = g_blocks.astype(BF16)
        lane = lax.broadcasted_iota(jnp.int32, (1, 2 * QN), 1)
        sink = jnp.exp(jnp.where(lane < QN, sink_ref[2 * p], sink_ref[2 * p + 1]))
        total = jnp.zeros((8, 2 * QN), F32)
        out = jnp.zeros((LANES, 2 * QN), F32)
        for c in range(N_CHUNK):
            here = slice(c * KEYS, (c + 1) * KEYS)
            k_here = ext[0, c * CHUNK : (c + 1) * CHUNK, span, :].reshape(KEYS, LANES)
            v_here = ext[1, c * CHUNK : (c + 1) * CHUNK, span, :].reshape(KEYS, LANES)
            squashed = jnp.tanh(dot(k_here, q_low))
            meets_here = mask[here, :]
            weight = jnp.exp2(squashed * EXP2_RATE) * jnp.concatenate([meets_here, meets_here], 1)
            total = total + jnp.sum(weight.reshape(KEYS // 8, 8, 2 * QN), axis=0)
            weight_low = weight.astype(BF16)
            e_s[here, :] = weight_low
            u_s[here, :] = (weight * (1.0 - squashed * squashed)).astype(BF16)
            out = out + dot(v_here, weight_low, TN)
        inverse = 1.0 / (jnp.sum(total, axis=0, keepdims=True) + sink)
        out = out * inverse
        delta = jnp.sum(g_blocks * out, axis=0, keepdims=True)
        out_s[0, p, :, cols, :] = own_heads(out).T.reshape(ROWS, TILE, LANES).astype(BF16)
        share = sink * inverse * delta
        sk[p, :, :] = sk[p, :, :] - jnp.concatenate([share[:, :QN], share[:, QN:]], 0)
        q_back = (q_blocks * (inverse * 0.125)).astype(BF16)
        g_back = (g_blocks * inverse).astype(BF16)
        dq = jnp.zeros((LANES, 2 * QN), F32)
        for c in range(N_CHUNK):
            here = slice(c * KEYS, (c + 1) * KEYS)
            rows = slice(c * CHUNK, (c + 1) * CHUNK)
            k_here = ext[0, rows, span, :].reshape(KEYS, LANES)
            v_here = ext[1, rows, span, :].reshape(KEYS, LANES)
            prob = dot(v_here, g_low) - delta
            score = (u_s[here, :].astype(F32) * prob).astype(BF16)
            dk = dot(score, q_back, NT)
            dv = dot(e_s[here, :], g_back, NT)
            dq = dq + dot(k_here, score, TN)
            acc[p, 0, rows, span, :] += dk.reshape(CHUNK, SPAN, LANES)
            acc[p, 1, rows, span, :] += dv.reshape(CHUNK, SPAN, LANES)
        dq = dq * (inverse * 0.125)
        out_s[1, p, :, cols, :] = own_heads(dq).T.reshape(ROWS, TILE, LANES).astype(BF16)

    def gs_copy(p, side):
        return pltpu.make_async_remote_copy(
            src_ref=gstrip_to.at[p, side],
            dst_ref=gstrip_from.at[p, 1 - side],
            send_sem=gs_send.at[p, side],
            recv_sem=gs_recv.at[p, 1 - side],
            device_id=sides[side],
            device_id_type=MESH,
        )

    def send_strips(p, side):
        first = (0, COLS + WIDE)[side]
        for rp in range(EXT_ROWS // 2):
            for i in range(2):
                both = acc[p, i, 2 * rp : 2 * rp + 2, first : first + WIDE, :]
                gstrip_to[p, side, rp, i] = both.reshape(2 * WIDE, LANES).astype(BF16)
        gs_copy(p, side).start()

    def rim_copy(p, side):
        return pltpu.make_async_remote_copy(
            src_ref=rim_to.at[p, side],
            dst_ref=rim_from.at[p, 1 - side],
            send_sem=rim_send.at[p, side],
            recv_sem=rim_recv.at[p, 1 - side],
            device_id=(up, down)[side],
            device_id_type=MESH,
        )

    def stage_c(p):
        for side in range(2):
            gs_copy(p, side).wait_recv()
        for rp in range(EXT_ROWS // 2):
            for i in range(2):
                for side in range(2):
                    first = (WIDE, COLS)[side]
                    came = gstrip_from[p, side, rp, i].astype(F32).reshape(2, WIDE, LANES)
                    acc[p, i, 2 * rp : 2 * rp + 2, first : first + WIDE, :] += came
        for i in range(2):
            for r in range(RADIUS):
                rim_to[p, 0, i, r] = acc[p, i, r, WIDE : WIDE + COLS, :].astype(BF16)
                rim_to[p, 1, i, r] = acc[p, i, RADIUS + ROWS + r, WIDE : WIDE + COLS, :].astype(BF16)
        for side in range(2):
            rim_copy(p, side).start()

    def store(i, p):
        return pltpu.make_async_copy(
            out_s.at[i, p],
            (o_hbm, dq_hbm, dk_hbm, dv_hbm)[i].at[
                :, :, pl.ds(pl.multiple_of(p * LANES, LANES), LANES)
            ],
            out_sem.at[i, p],
        )

    def stage_d(p):
        for side in range(2):
            rim_copy(p, side).wait_recv()
        for i in range(2):
            for r in range(ROWS):
                total = acc[p, i, RADIUS + r, WIDE : WIDE + COLS, :]
                if r < RADIUS:
                    total = total + rim_from[p, 0, i, r].astype(F32)
                if r >= ROWS - RADIUS:
                    total = total + rim_from[p, 1, i, r - (ROWS - RADIUS)].astype(F32)
                out_s[2 + i, p, r] = total.astype(BF16)
        for i in (2, 3):
            store(i, p).start()

    sk[...] = jnp.zeros_like(sk)
    stage_a(0)

    def step(p, carry):
        for i in (0, 3):
            load(i, p).wait()
        stage_ext(p)
        attend(p, 0)
        send_strips(p, 0)

        @pl.when(p < PAIRS - 1)
        def _():
            stage_a(p + 1)

        @pl.when(p > 0)
        def _():
            stage_c(p - 1)

        attend(p, 1)
        send_strips(p, 1)
        for i in (0, 1):
            store(i, p).start()

        @pl.when(p > 1)
        def _():
            stage_d(p - 2)

        return carry

    lax.fori_loop(0, PAIRS, step, 0)

    groups = ((N_LAT, lat_peer), (4, quad_peer), (N_Z, z_peer))

    def sk_copy(stage, d):
        size, peer = groups[stage]
        return pltpu.make_async_remote_copy(
            src_ref=sk_all.at[stage, 0],
            dst_ref=sk_all.at[stage, d],
            send_sem=sk_send.at[stage, d],
            recv_sem=sk_recv.at[stage, d],
            device_id=peer(d),
            device_id_type=MESH,
        )

    def sk_put(stage):
        for d in range(1, groups[stage][0]):
            sk_copy(stage, d).start()

    def sk_get(stage):
        for d in range(1, groups[stage][0]):
            sk_copy(stage, d).wait_recv()
        return jnp.sum(sk_all[stage, : groups[stage][0]], axis=0)

    sk_all[0, 0] = sk[...].reshape(2 * PAIRS, QN)
    sk_put(0)
    stage_c(PAIRS - 1)
    stage_d(PAIRS - 2)
    sk_all[1, 0] = sk_get(0)
    sk_put(1)
    sk_all[2, 0] = sk_get(1)

    @pl.when(z < N_Z - 1)
    def _():
        pl.semaphore_wait(met, N_Z - 1 - z)

    sk_put(2)
    stage_d(PAIRS - 1)
    sg_ref[...] = jnp.broadcast_to(jnp.sum(sk_get(2), axis=1, keepdims=True), (2 * PAIRS, QN))

    for p in range(PAIRS):
        for i in range(4):
            store(i, p).wait()
        for side in range(2):
            for i in range(2):
                lat_copy(p, i, side).wait_send()
            for part in range(3):
                strip_copy(p, side, part).wait_send()
            gs_copy(p, side).wait_send()
            rim_copy(p, side).wait_send()
    for stage in range(3):
        for d in range(1, groups[stage][0]):
            sk_copy(stage, d).wait_send()


def on_device(queries, keys, values, grad_out, sink_logits):
    shape = jax.ShapeDtypeStruct(queries.shape, BF16)
    anywhere = pl.BlockSpec(memory_space=pl.ANY)
    dma = pltpu.SemaphoreType.DMA
    attended, query_grad, key_grad, value_grad, sink_grad = pl.pallas_call(
        kernel,
        out_shape=(shape,) * 4 + (jax.ShapeDtypeStruct((2 * PAIRS, QN), F32),),
        in_specs=[anywhere] * 4 + [pl.BlockSpec(memory_space=pltpu.SMEM)],
        out_specs=(anywhere,) * 4 + (pl.BlockSpec(memory_space=pltpu.VMEM),),
        scratch_shapes=[
            pltpu.VMEM((PAIRS, ROWS, COLS, LANES), BF16),
            pltpu.VMEM((2, PAIRS, ROWS, COLS, LANES), BF16),
            pltpu.VMEM((PAIRS, ROWS, COLS, LANES), BF16),
            pltpu.VMEM((2, EXT_ROWS, EXT_COLS, LANES), BF16),
            pltpu.VMEM((PAIRS, 2, RADIUS, COLS, LANES), BF16),
            pltpu.VMEM((PAIRS, 2, RADIUS, COLS, LANES), BF16),
            pltpu.VMEM((EXT_ROWS * SPAN, QN), F32),
            pltpu.VMEM((PAIRS, 2, EXT_ROWS // 2, 2, 2 * WIDE, LANES), BF16),
            pltpu.VMEM((PAIRS, 2, EXT_ROWS // 2, 2, 2 * WIDE, LANES), BF16),
            pltpu.VMEM((PAIRS, 2, EXT_ROWS // 2, 2, 2 * WIDE, LANES), BF16),
            pltpu.VMEM((PAIRS, 2, EXT_ROWS // 2, 2, 2 * WIDE, LANES), BF16),
            pltpu.VMEM((PAIRS, 2, 2, RADIUS, COLS, LANES), BF16),
            pltpu.VMEM((PAIRS, 2, 2, RADIUS, COLS, LANES), BF16),
            pltpu.VMEM((PAIRS, 2, EXT_ROWS, EXT_COLS, LANES), F32),
            pltpu.VMEM((EXT_ROWS * SPAN, 2 * QN), BF16),
            pltpu.VMEM((EXT_ROWS * SPAN, 2 * QN), BF16),
            pltpu.VMEM((4, PAIRS, ROWS, COLS, LANES), BF16),
            pltpu.VMEM((PAIRS, 2, QN), F32),
            pltpu.VMEM((3, N_LAT, 2 * PAIRS, QN), F32),
            dma((4, PAIRS)),
            dma((4, PAIRS)),
            dma((PAIRS, 2, 2)),
            dma((PAIRS, 2, 2)),
            dma((PAIRS, 2, 3)),
            dma((PAIRS, 2, 3)),
            dma((PAIRS, 2)),
            dma((PAIRS, 2)),
            dma((PAIRS, 2)),
            dma((PAIRS, 2)),
            dma((3, N_LAT)),
            dma((3, N_LAT)),
            pltpu.SemaphoreType.REGULAR((2,)),
            pltpu.SemaphoreType.REGULAR,
        ],
        compiler_params=pltpu.CompilerParams(
            collective_id=0, has_side_effects=True, vmem_limit_bytes=60 * 1024 * 1024
        ),
    )(queries, keys, values, grad_out, sink_logits)
    return attended, query_grad, key_grad, value_grad, sink_grad[:, 0]


def solution(mesh):
    cells = P("lat", "lon", None)
    return jax.shard_map(
        on_device,
        mesh=mesh,
        in_specs=(cells,) * 4 + (P(),),
        out_specs=(cells,) * 4 + (P(),),
        check_vma=False,
    )
```

```python
import functools
import math

import jax
import jax.numpy as jnp
from jax import lax
from jax.experimental import pallas as pl
from jax.experimental.pallas import tpu as pltpu
from jax.sharding import PartitionSpec as P

WIN = 13
RADIUS = WIN // 2
SOFTCAP = 8.0
PAIRS = 4
ROWS = 8
COLS = 32
WIDE = 8
EXT_ROWS = ROWS + 2 * RADIUS
EXT_COLS = COLS + 2 * WIDE
TILE = 16
SPAN = TILE + 2 * WIDE
KEYS = EXT_ROWS * SPAN
QN = ROWS * TILE
LANES = 128
N_LAT = 8
N_LON = 32
N_Z = 8
N_NEAR = 2 * N_LAT
N_FAR = 2 * N_Z
MESH = pl.DeviceIdType.MESH
BF16 = jnp.bfloat16
F32 = jnp.float32
EXP2_RATE = SOFTCAP * math.log2(math.e)

NT = (((1,), (1,)), ((), ()))
TN = (((0,), (0,)), ((), ()))


def dot(a, b, dims=(((1,), (0,)), ((), ()))):
    return lax.dot_general(a, b, dims, preferred_element_type=F32)


def head_blocks(turned):
    first = lax.broadcasted_iota(jnp.int32, (LANES, QN), 0) < LANES // 2
    return jnp.concatenate(
        [jnp.where(first, turned, 0.0), jnp.where(first, 0.0, turned)], axis=1
    )


def own_heads(both):
    first = lax.broadcasted_iota(jnp.int32, (LANES, QN), 0) < LANES // 2
    return jnp.where(first, both[:, :QN], both[:, QN:])


def kernel(
    q_hbm, k_hbm, v_hbm, g_hbm, sink_hbm,
    o_ref, dq_ref, dk_ref, dv_ref, sg_ref,
    sink_ref, q_s, kv_s, g_s, ext, top, bot, mask,
    strip_to, strip_from, gstrip_to, gstrip_from, rim_to, rim_from,
    acc, e_s, u_s, prob_s, rate, sk, sk_plane, sk_z,
    sink_sem, in_sem, lat_send, lat_recv, strip_send, strip_recv,
    gs_send, gs_recv, rim_send, rim_recv, skp_send, skp_recv, skz_send, skz_recv, entered, met,
):
    a = lax.axis_index("lat")
    b = lax.axis_index("lon")
    up = (lax.rem(a + N_LAT - 1, N_LAT), b)
    down = (lax.rem(a + 1, N_LAT), b)
    left = (a, lax.rem(b + N_LON - 1, N_LON))
    right = (a, lax.rem(b + 1, N_LON))
    sides = (left, right)
    column = lax.rem(b, 2 * N_Z)
    z = column // 2
    is_first = column == 0
    is_last = column == 2 * N_Z - 1

    core = lax.rem(b, 2)
    crossing = (left[1], right[1])

    def diagonal(side, da):
        return (lax.rem(a + da + N_LAT, N_LAT), crossing[side])

    half = b // (2 * N_Z)

    def near_peer(d):
        other = lax.rem(2 * a + core + d, N_NEAR)
        return (other // 2, lax.rem(other, 2) + 2 * z + 2 * N_Z * half)

    def across(dz, dh):
        return (a, core + 2 * lax.rem(z + dz + N_Z, N_Z) + 2 * N_Z * lax.rem(half + dh, 2))

    def far_peer(d):
        other = lax.rem(2 * z + half + d, N_FAR)
        return (a, core + 2 * (other // 2) + 2 * N_Z * lax.rem(other, 2))

    def load(i, p):
        src = (q_hbm, k_hbm, v_hbm, g_hbm)[i]
        dst = (q_s, kv_s.at[0], kv_s.at[1], g_s)[i]
        return pltpu.make_async_copy(
            src.at[:, :, pl.ds(pl.multiple_of(p * LANES, LANES), LANES)], dst.at[p], in_sem.at[i, p]
        )

    for p in range(PAIRS):
        for i in (1, 2):
            load(i, p).start()
    for p in range(PAIRS):
        for i in (0, 3):
            load(i, p).start()

    sink_copy = pltpu.make_async_copy(sink_hbm, sink_ref, sink_sem)
    sink_copy.start()
    barrier = pltpu.get_barrier_semaphore()

    def greet(device):
        pl.semaphore_signal(barrier, inc=1, device_id=device, device_id_type=MESH)

    for d in range(1, N_NEAR):
        greet(near_peer(d))
    greet(across(0, 1))

    @pl.when((core == 1) & jnp.logical_not(is_last))
    def _():
        greet(right)

    @pl.when(is_first)
    def _():
        for da in (-1, 0, 1):
            greet(diagonal(0, da))

    for d in range(1, N_Z):
        @pl.when(z + d < N_Z)
        def _():
            greet(across(d, 0))
            greet(across(d, 1))

    answers = ((core == 0) & jnp.logical_not(is_first)) | is_last
    pl.semaphore_wait(barrier, N_NEAR + 2 * z + jnp.where(is_last, 3, jnp.where(answers, 1, 0)))

    def lat_copy(p, i, side):
        src = (k_hbm, v_hbm)[i]
        first_row = (0, ROWS - RADIUS)[side]
        return pltpu.make_async_remote_copy(
            src_ref=src.at[
                first_row : first_row + RADIUS, :, pl.ds(pl.multiple_of(p * LANES, LANES), LANES)
            ],
            dst_ref=(bot, top)[side].at[p, i],
            send_sem=lat_send.at[p, i, side],
            recv_sem=lat_recv.at[p, i, side],
            device_id=(up, down)[side],
            device_id_type=MESH,
        )

    def send_rows(p):
        for i in range(2):
            for side in range(2):
                lat_copy(p, i, side).start()

    send_rows(0)
    send_rows(1)

    @pl.when((core == 0) & jnp.logical_not(is_first))
    def _():
        pl.semaphore_signal(entered, inc=1, device_id=left, device_id_type=MESH)

    @pl.when(is_last)
    def _():
        for da in (-1, 0, 1):
            pl.semaphore_signal(entered, inc=1, device_id=diagonal(1, da), device_id_type=MESH)

    for d in range(1, N_Z):
        @pl.when(z - d >= 0)
        def _():
            for dh in range(2):
                pl.semaphore_signal(met, inc=1, device_id=across(-d, dh), device_id_type=MESH)

    key = lax.broadcasted_iota(jnp.int32, (EXT_ROWS * SPAN, QN), 0)
    query = lax.broadcasted_iota(jnp.int32, (EXT_ROWS * SPAN, QN), 1)
    key_row = key // SPAN - RADIUS
    row_gap = key_row - query // TILE
    col_gap = lax.rem(key, SPAN) - WIDE - lax.rem(query, TILE)
    whole_row = a * ROWS + key_row
    meets = (
        (row_gap >= -RADIUS) & (row_gap <= RADIUS) & (col_gap >= -RADIUS) & (col_gap <= RADIUS)
        & (whole_row >= 0) & (whole_row < N_LAT * ROWS)
    )
    mask[...] = jnp.where(meets, 1.0, 0.0)

    def rows_of(p, i, r):
        if r < RADIUS:
            return top[p, i, r].astype(F32)
        if r < RADIUS + ROWS:
            return kv_s[i, p, r - RADIUS].astype(F32)
        return bot[p, i, r - RADIUS - ROWS].astype(F32)

    def pack(p, first, last):
        for rp in range(first, last):
            for i in range(2):
                upper, lower = rows_of(p, i, 2 * rp), rows_of(p, i, 2 * rp + 1)
                strip_to[p, 0, rp, i] = jnp.concatenate([upper[:WIDE], lower[:WIDE]], 0).astype(BF16)
                strip_to[p, 1, rp, i] = jnp.concatenate(
                    [upper[COLS - WIDE :], lower[COLS - WIDE :]], 0
                ).astype(BF16)

    spans = ((3, 4), (0, 3), (7, 3))
    direct = (is_first, is_last)

    def strip_copy(p, side, part):
        first, count = spans[part]
        source, to = first, a
        if part == 1:
            source, to = jnp.where(direct[side], 4, 0), jnp.where(direct[side], lax.rem(a + 1, N_LAT), a)
        if part == 2:
            source = jnp.where(direct[side], 3, 7)
            to = jnp.where(direct[side], lax.rem(a + N_LAT - 1, N_LAT), a)
        return pltpu.make_async_remote_copy(
            src_ref=strip_to.at[p, side, pl.ds(source, count)],
            dst_ref=strip_from.at[p, 1 - side, first : first + count],
            send_sem=strip_send.at[p, side, part],
            recv_sem=strip_recv.at[p, 1 - side, part],
            device_id=(to, sides[side][1]),
            device_id_type=MESH,
        )

    for p in range(PAIRS):
        for i in (1, 2):
            load(i, p).wait()
        pack(p, 3, 7)

    @pl.when(is_last)
    def _():
        for p in range(PAIRS):
            for part in (1, 2):
                strip_copy(p, 1, part).start()

    send_rows(2)
    send_rows(3)
    sure = ((core == 1) | (core == 0) & jnp.logical_not(is_first), (core == 0) | is_last)
    for side in range(2):
        @pl.when(sure[side])
        def _():
            for p in range(PAIRS):
                strip_copy(p, side, 0).start()

    acc[...] = jnp.zeros_like(acc)
    sk[...] = jnp.zeros_like(sk)

    def stage_a(p):
        for i in range(2):
            for side in range(2):
                lat_copy(p, i, side).wait_recv()
        pack(p, 0, 3)
        pack(p, 7, 10)
        for side in range(2):
            @pl.when(jnp.logical_not(direct[side]))
            def _():
                for part in (1, 2):
                    strip_copy(p, side, part).start()

    def ext_middle(p):
        for r in range(EXT_ROWS):
            for i in range(2):
                ext[i, r, TILE : 2 * TILE] = rows_of(p, i, r)[WIDE : WIDE + TILE].astype(BF16)

    def ext_sides(p):
        for side in range(2):
            for part in range(3):
                strip_copy(p, side, part).wait_recv()
        for rp in range(EXT_ROWS // 2):
            for i in range(2):
                west = strip_from[p, 0, rp, i].astype(F32)
                east = strip_from[p, 1, rp, i].astype(F32)
                for j in range(2):
                    r = 2 * rp + j
                    half = slice(j * WIDE, (j + 1) * WIDE)
                    center = rows_of(p, i, r)
                    ext[i, r, :TILE] = jnp.concatenate([west[half], center[:WIDE]], 0).astype(BF16)
                    ext[i, r, 2 * TILE :] = jnp.concatenate(
                        [center[COLS - WIDE :], east[half]], 0
                    ).astype(BF16)

    def place(tile):
        at = tile * TILE
        return slice(at, at + TILE), slice(at, at + SPAN)

    def lanes(p):
        return pl.ds(pl.multiple_of(p * LANES, LANES), LANES)

    def turned(ref, p, cols):
        return head_blocks(ref[p, :, cols, :].reshape(QN, LANES).astype(F32).T)

    def forward(p, tile):
        cols, span = place(tile)
        q_low = (turned(q_s, p, cols) * (1.0 / 64.0)).astype(BF16)
        lane = lax.broadcasted_iota(jnp.int32, (1, 2 * QN), 1)
        sink = jnp.exp(jnp.where(lane < QN, sink_ref[2 * p], sink_ref[2 * p + 1]))
        k_here = ext[0, :, span, :].reshape(KEYS, LANES)
        v_here = ext[1, :, span, :].reshape(KEYS, LANES)
        g_blocks = turned(g_s, p, cols)
        squashed = jnp.tanh(dot(k_here, q_low))
        meets_here = mask[...]
        weight = jnp.exp2(squashed * EXP2_RATE) * jnp.concatenate([meets_here, meets_here], 1)
        total = jnp.sum(weight.reshape(KEYS // 8, 8, 2 * QN), axis=0)
        weight_low = weight.astype(BF16)
        e_s[tile] = weight_low
        u_s[tile] = (weight * (1.0 - squashed * squashed)).astype(BF16)
        prob_s[tile] = dot(v_here, g_blocks.astype(BF16))
        out = dot(v_here, weight_low, TN)
        inverse = 1.0 / (jnp.sum(total, axis=0, keepdims=True) + sink)
        out = out * inverse
        delta = jnp.sum(g_blocks * out, axis=0, keepdims=True)
        rate[tile, 0] = jnp.broadcast_to(inverse, (8, 2 * QN))
        rate[tile, 1] = jnp.broadcast_to(delta, (8, 2 * QN))
        o_ref[:, cols, lanes(p)] = own_heads(out).T.reshape(ROWS, TILE, LANES).astype(BF16)
        share = sink * inverse * delta
        sk[p, :, :] = sk[p, :, :] - jnp.concatenate([share[:, :QN], share[:, QN:]], 0)

    def backward(p, tile):
        cols, span = place(tile)
        inverse = rate[tile, 0, 0:1, :]
        delta = rate[tile, 1, 0:1, :]
        g_blocks = turned(g_s, p, cols)
        q_back = (turned(q_s, p, cols) * (inverse * 0.125)).astype(BF16)
        g_back = (g_blocks * inverse).astype(BF16)
        k_here = ext[0, :, span, :].reshape(KEYS, LANES)
        score = (u_s[tile].astype(F32) * (prob_s[tile] - delta)).astype(BF16)
        dk = dot(score, q_back, NT)
        dv = dot(e_s[tile], g_back, NT)
        dq = dot(k_here, score, TN)
        acc[p, 0, :, span, :] += dk.reshape(EXT_ROWS, SPAN, LANES)
        acc[p, 1, :, span, :] += dv.reshape(EXT_ROWS, SPAN, LANES)
        dq = dq * (inverse * 0.125)
        dq_ref[:, cols, lanes(p)] = own_heads(dq).T.reshape(ROWS, TILE, LANES).astype(BF16)

    def gs_copy(p, side, part):
        first, count = spans[part]
        to, lands = a, first
        if part == 1:
            to = jnp.where(direct[side], lax.rem(a + N_LAT - 1, N_LAT), a)
            lands = jnp.where(direct[side], 7, 0)
        if part == 2:
            to = jnp.where(direct[side], lax.rem(a + 1, N_LAT), a)
            lands = jnp.where(direct[side], 0, 7)
        sem = part if part == 0 else jnp.where(direct[side], 3 - part, part)
        return pltpu.make_async_remote_copy(
            src_ref=gstrip_to.at[p, side, first : first + count],
            dst_ref=gstrip_from.at[p, 1 - side, pl.ds(lands, count)],
            send_sem=gs_send.at[p, side, sem],
            recv_sem=gs_recv.at[p, 1 - side, sem],
            device_id=(to, sides[side][1]),
            device_id_type=MESH,
        )

    def send_strips(p, side):
        first = side * (COLS + WIDE)
        for rp in range(EXT_ROWS // 2):
            for i in range(2):
                both = acc[p, i, 2 * rp : 2 * rp + 2, first : first + WIDE, :]
                gstrip_to[p, side, rp, i] = both.reshape(2 * WIDE, LANES).astype(BF16)

    def start_strips(p):
        for side in range(2):
            for part in (1, 2, 0):
                gs_copy(p, side, part).start()

    def rim_copy(p, side):
        return pltpu.make_async_remote_copy(
            src_ref=rim_to.at[p, side],
            dst_ref=rim_from.at[p, 1 - side],
            send_sem=rim_send.at[p, side],
            recv_sem=rim_recv.at[p, 1 - side],
            device_id=(up, down)[side],
            device_id_type=MESH,
        )

    def add_strip(p, side, rp, row):
        first = (WIDE, COLS)[side]
        for i in range(2):
            came = gstrip_from[p, side, rp, i].astype(F32).reshape(2, WIDE, LANES)
            acc[p, i, pl.ds(row, 2), first : first + WIDE, :] += came

    def stage_c(p):
        for side in range(2):
            @pl.when(jnp.logical_not(direct[side]))
            def _():
                for part in (1, 2):
                    gs_copy(p, 1 - side, part).wait_recv()
                for rp in (0, 1, 2, 7, 8, 9):
                    add_strip(p, side, rp, 2 * rp)
        for i in range(2):
            for r in range(RADIUS):
                rim_to[p, 0, i, r] = acc[p, i, r, WIDE : WIDE + COLS, :].astype(BF16)
                rim_to[p, 1, i, r] = acc[p, i, RADIUS + ROWS + r, WIDE : WIDE + COLS, :].astype(BF16)
        for side in range(2):
            rim_copy(p, side).start()

    def stage_d(p):
        for side in range(2):
            gs_copy(p, 1 - side, 0).wait_recv()
            for rp in (3, 4, 5, 6):
                add_strip(p, side, rp, 2 * rp)

            @pl.when(direct[side])
            def _():
                for part in (1, 2):
                    gs_copy(p, 1 - side, part).wait_recv()
                for rp in range(3):
                    add_strip(p, side, rp, 2 * rp + RADIUS)
                    add_strip(p, side, rp + 7, 2 * rp + RADIUS + 2)
        for side in range(2):
            rim_copy(p, side).wait_recv()
        for i in range(2):
            for r in range(ROWS):
                total = acc[p, i, RADIUS + r, WIDE : WIDE + COLS, :]
                if r < RADIUS:
                    total = total + rim_from[p, 0, i, r].astype(F32)
                if r >= ROWS - RADIUS:
                    total = total + rim_from[p, 1, i, r - (ROWS - RADIUS)].astype(F32)
                (dk_ref, dv_ref)[i][r, :, lanes(p)] = total.astype(BF16)

    def skp_copy(d):
        return pltpu.make_async_remote_copy(
            src_ref=sk_plane.at[0], dst_ref=sk_plane.at[d],
            send_sem=skp_send.at[d], recv_sem=skp_recv.at[d],
            device_id=near_peer(d), device_id_type=MESH,
        )

    def skz_copy(d):
        return pltpu.make_async_remote_copy(
            src_ref=sk_z.at[0], dst_ref=sk_z.at[d],
            send_sem=skz_send.at[d], recv_sem=skz_recv.at[d],
            device_id=far_peer(d), device_id_type=MESH,
        )

    sink_copy.wait()

    @pl.when((core == 1) & jnp.logical_not(is_last))
    def _():
        pl.semaphore_wait(entered, 1)
        for p in range(PAIRS):
            strip_copy(p, 1, 0).start()

    stage_a(0)
    stage_a(1)

    @pl.when(is_first)
    def _():
        pl.semaphore_wait(entered, 3)
        for p in range(PAIRS):
            for part in (1, 2, 0):
                strip_copy(p, 0, part).start()
        stage_a(2)
        stage_a(3)

    def gather(p):
        for i in (0, 3):
            load(i, p).wait()
        ext_middle(p)
        ext_sides(p)

    def forward_both(p):
        forward(p, 0)
        forward(p, 1)

    def backward_both(p):
        backward(p, 0)
        backward(p, 1)
        send_strips(p, 0)
        send_strips(p, 1)
        start_strips(p)

    def step(p, carry):
        gather(p)
        forward_both(p)
        backward_both(p)

        @pl.when((p < PAIRS - 2) & jnp.logical_not(is_first))
        def _():
            stage_a(p + 2)

        @pl.when(p > 0)
        def _():
            stage_c(p - 1)

        return carry

    lax.fori_loop(0, PAIRS - 1, step, 0)
    gather(PAIRS - 1)
    forward_both(PAIRS - 1)
    sk_plane[0] = sk[...].reshape(2 * PAIRS, QN)
    for d in range(1, N_NEAR):
        skp_copy(d).start()
    backward_both(PAIRS - 1)
    stage_c(PAIRS - 2)
    stage_c(PAIRS - 1)
    for d in range(1, N_NEAR):
        skp_copy(d).wait_recv()
    sk_z[0] = jnp.sum(sk_plane[...], axis=0)

    @pl.when(z < N_Z - 1)
    def _():
        pl.semaphore_wait(met, 2 * (N_Z - 1 - z))

    for d in range(1, N_FAR):
        skz_copy(d).start()

    def finish(p, carry):
        stage_d(p)
        return carry

    lax.fori_loop(0, PAIRS, finish, 0)
    for d in range(1, N_FAR):
        skz_copy(d).wait_recv()
    sg_ref[...] = jnp.broadcast_to(
        jnp.sum(jnp.sum(sk_z[...], axis=0), axis=1, keepdims=True), (2 * PAIRS, QN)
    )

    for p in range(PAIRS):
        for side in range(2):
            for i in range(2):
                lat_copy(p, i, side).wait_send()
            for part in range(3):
                strip_copy(p, side, part).wait_send()
                gs_copy(p, side, part).wait_send()
            rim_copy(p, side).wait_send()
    for d in range(1, N_NEAR):
        skp_copy(d).wait_send()
    for d in range(1, N_FAR):
        skz_copy(d).wait_send()


def place_results(o_ref, dq_ref, dk_ref, dv_ref, sg_ref, o_out, dq_out, dk_out, dv_out, sg_out, sem):
    sources = (o_ref, dq_ref, dk_ref, dv_ref)
    stores = [
        pltpu.make_async_copy(sources[i], there, sem.at[i])
        for i, there in enumerate((o_out, dq_out, dk_out, dv_out))
    ]
    for store in stores:
        store.start()
    row = lax.broadcasted_iota(jnp.int32, (2 * PAIRS, QN), 0)
    lane = lax.broadcasted_iota(jnp.int32, (2 * PAIRS, QN), 1)
    sg_out[...] = jnp.sum(jnp.where(row == lane, sg_ref[...], 0.0), axis=0)[: 2 * PAIRS]
    for store in stores:
        store.wait()


def on_device(queries, keys, values, grad_out, sink_logits):
    shape = jax.ShapeDtypeStruct(queries.shape, BF16)
    anywhere = pl.BlockSpec(memory_space=pl.ANY)
    dma = pltpu.SemaphoreType.DMA
    vmem = pl.BlockSpec(memory_space=pltpu.VMEM)
    results = pl.pallas_call(
        kernel,
        out_shape=(pltpu.VMEM(queries.shape, BF16),) * 4 + (pltpu.VMEM((2 * PAIRS, QN), F32),),
        in_specs=[anywhere] * 5,
        out_specs=(vmem,) * 5,
        scratch_shapes=[
            pltpu.SMEM((2 * PAIRS,), F32),
            pltpu.VMEM((PAIRS, ROWS, COLS, LANES), BF16),
            pltpu.VMEM((2, PAIRS, ROWS, COLS, LANES), BF16),
            pltpu.VMEM((PAIRS, ROWS, COLS, LANES), BF16),
            pltpu.VMEM((2, EXT_ROWS, EXT_COLS, LANES), BF16),
            pltpu.VMEM((PAIRS, 2, RADIUS, COLS, LANES), BF16),
            pltpu.VMEM((PAIRS, 2, RADIUS, COLS, LANES), BF16),
            pltpu.VMEM((EXT_ROWS * SPAN, QN), F32),
            pltpu.VMEM((PAIRS, 2, EXT_ROWS // 2, 2, 2 * WIDE, LANES), BF16),
            pltpu.VMEM((PAIRS, 2, EXT_ROWS // 2, 2, 2 * WIDE, LANES), BF16),
            pltpu.VMEM((PAIRS, 2, EXT_ROWS // 2, 2, 2 * WIDE, LANES), BF16),
            pltpu.VMEM((PAIRS, 2, EXT_ROWS // 2, 2, 2 * WIDE, LANES), BF16),
            pltpu.VMEM((PAIRS, 2, 2, RADIUS, COLS, LANES), BF16),
            pltpu.VMEM((PAIRS, 2, 2, RADIUS, COLS, LANES), BF16),
            pltpu.VMEM((PAIRS, 2, EXT_ROWS, EXT_COLS, LANES), F32),
            pltpu.VMEM((2, EXT_ROWS * SPAN, 2 * QN), BF16),
            pltpu.VMEM((2, EXT_ROWS * SPAN, 2 * QN), BF16),
            pltpu.VMEM((2, EXT_ROWS * SPAN, 2 * QN), F32),
            pltpu.VMEM((2, 2, 8, 2 * QN), F32),
            pltpu.VMEM((PAIRS, 2, QN), F32),
            pltpu.VMEM((N_NEAR, 2 * PAIRS, QN), F32),
            pltpu.VMEM((N_FAR, 2 * PAIRS, QN), F32),
            dma(()),
            dma((4, PAIRS)),
            dma((PAIRS, 2, 2)),
            dma((PAIRS, 2, 2)),
            dma((PAIRS, 2, 3)),
            dma((PAIRS, 2, 3)),
            dma((PAIRS, 2, 3)),
            dma((PAIRS, 2, 3)),
            dma((PAIRS, 2)),
            dma((PAIRS, 2)),
            dma((N_NEAR,)),
            dma((N_NEAR,)),
            dma((N_FAR,)),
            dma((N_FAR,)),
            pltpu.SemaphoreType.REGULAR,
            pltpu.SemaphoreType.REGULAR,
        ],
        compiler_params=pltpu.CompilerParams(
            collective_id=0, has_side_effects=True, vmem_limit_bytes=60 * 1024 * 1024
        ),
    )(queries, keys, values, grad_out, sink_logits)
    results = [pltpu.with_memory_space_constraint(result, pltpu.VMEM) for result in results]
    return pl.pallas_call(
        place_results,
        out_shape=(shape,) * 4 + (jax.ShapeDtypeStruct((2 * PAIRS,), F32),),
        in_specs=[anywhere] * 4 + [vmem],
        out_specs=(anywhere,) * 4 + (vmem,),
        scratch_shapes=[dma((4,))],
    )(*results)


def solution(mesh):
    cells = P("lat", "lon", None)
    return jax.shard_map(
        on_device,
        mesh=mesh,
        in_specs=(cells,) * 4 + (P(),),
        out_specs=(cells,) * 4 + (P(),),
        check_vma=False,
    )
```

```python
import functools
import math

import jax
import jax.numpy as jnp
from jax import lax
from jax.experimental import pallas as pl
from jax.experimental.pallas import tpu as pltpu
from jax.sharding import PartitionSpec as P

WIN = 13
RADIUS = WIN // 2
SOFTCAP = 8.0
PAIRS = 4
ROWS = 8
COLS = 32
WIDE = 8
CORNERS_FIRST = 2
EXT_ROWS = ROWS + 2 * RADIUS
EXT_COLS = COLS + 2 * WIDE
TILE = 16
SPAN = TILE + 2 * WIDE
KEYS = EXT_ROWS * SPAN
QN = ROWS * TILE
LANES = 128
N_LAT = 8
N_LON = 32
N_Z = 8
N_NEAR = 2 * N_LAT
N_FAR = 2 * N_Z
MESH = pl.DeviceIdType.MESH
BF16 = jnp.bfloat16
F32 = jnp.float32
EXP2_RATE = SOFTCAP * math.log2(math.e)

NT = (((1,), (1,)), ((), ()))
TN = (((0,), (0,)), ((), ()))


def dot(a, b, dims=(((1,), (0,)), ((), ()))):
    return lax.dot_general(a, b, dims, preferred_element_type=F32)


def head_blocks(turned):
    first = lax.broadcasted_iota(jnp.int32, (LANES, QN), 0) < LANES // 2
    return jnp.concatenate(
        [jnp.where(first, turned, 0.0), jnp.where(first, 0.0, turned)], axis=1
    )


def own_heads(both):
    first = lax.broadcasted_iota(jnp.int32, (LANES, QN), 0) < LANES // 2
    return jnp.where(first, both[:, :QN], both[:, QN:])


def kernel(
    q_hbm, k_hbm, v_hbm, g_hbm, sink_hbm,
    o_ref, dq_ref, dk_ref, dv_ref, sg_ref,
    sink_ref, q_s, kv_s, g_s, ext, top, bot, mask,
    strip_to, strip_from, gstrip_to, gstrip_from, rim_to, rim_from,
    acc, e_s, u_s, prob_s, rate, sk, sk_plane, sk_z,
    sink_sem, in_sem, lat_send, lat_recv, strip_send, strip_recv,
    gs_send, gs_recv, rim_send, rim_recv, skp_send, skp_recv, skz_send, skz_recv, entered, met,
):
    a = lax.axis_index("lat")
    b = lax.axis_index("lon")
    up = (lax.rem(a + N_LAT - 1, N_LAT), b)
    down = (lax.rem(a + 1, N_LAT), b)
    left = (a, lax.rem(b + N_LON - 1, N_LON))
    right = (a, lax.rem(b + 1, N_LON))
    sides = (left, right)
    column = lax.rem(b, 2 * N_Z)
    z = column // 2
    is_first = column == 0
    is_last = column == 2 * N_Z - 1

    core = lax.rem(b, 2)
    crossing = (left[1], right[1])

    def diagonal(side, da):
        return (lax.rem(a + da + N_LAT, N_LAT), crossing[side])

    half = b // (2 * N_Z)

    def near_peer(d):
        other = lax.rem(2 * a + core + d, N_NEAR)
        return (other // 2, lax.rem(other, 2) + 2 * z + 2 * N_Z * half)

    def across(dz, dh):
        return (a, core + 2 * lax.rem(z + dz + N_Z, N_Z) + 2 * N_Z * lax.rem(half + dh, 2))

    def far_peer(d):
        other = lax.rem(2 * z + half + d, N_FAR)
        return (a, core + 2 * (other // 2) + 2 * N_Z * lax.rem(other, 2))

    def load(i, p):
        src = (q_hbm, k_hbm, v_hbm, g_hbm)[i]
        dst = (q_s, kv_s.at[0], kv_s.at[1], g_s)[i]
        return pltpu.make_async_copy(
            src.at[:, :, pl.ds(pl.multiple_of(p * LANES, LANES), LANES)], dst.at[p], in_sem.at[i, p]
        )

    for p in range(PAIRS):
        for i in (1, 2):
            load(i, p).start()
    for p in range(PAIRS):
        for i in (0, 3):
            load(i, p).start()

    sink_copy = pltpu.make_async_copy(sink_hbm, sink_ref, sink_sem)
    sink_copy.start()
    barrier = pltpu.get_barrier_semaphore()

    def greet(device):
        pl.semaphore_signal(barrier, inc=1, device_id=device, device_id_type=MESH)

    for d in range(1, N_NEAR):
        greet(near_peer(d))
    greet(across(0, 1))

    @pl.when((core == 1) & jnp.logical_not(is_last))
    def _():
        greet(right)

    @pl.when(is_first)
    def _():
        for da in (-1, 0, 1):
            greet(diagonal(0, da))

    for d in range(1, N_Z):
        @pl.when(z + d < N_Z)
        def _():
            greet(across(d, 0))
            greet(across(d, 1))

    def rows_of(p, i, r):
        if r < RADIUS:
            return top[p, i, r].astype(F32)
        if r < RADIUS + ROWS:
            return kv_s[i, p, r - RADIUS].astype(F32)
        return bot[p, i, r - RADIUS - ROWS].astype(F32)

    def pack(p, first, last):
        for rp in range(first, last):
            for i in range(2):
                upper, lower = rows_of(p, i, 2 * rp), rows_of(p, i, 2 * rp + 1)
                strip_to[p, 0, rp, i] = jnp.concatenate([upper[:WIDE], lower[:WIDE]], 0).astype(BF16)
                strip_to[p, 1, rp, i] = jnp.concatenate(
                    [upper[COLS - WIDE :], lower[COLS - WIDE :]], 0
                ).astype(BF16)

    spans = ((3, 4), (0, 3), (7, 3))

    direct = (is_first, is_last)

    def strip_copy(p, side, part):
        first, count = spans[part]
        source, to = first, a
        if part == 1:
            source, to = jnp.where(direct[side], 4, 0), jnp.where(direct[side], lax.rem(a + 1, N_LAT), a)
        if part == 2:
            source = jnp.where(direct[side], 3, 7)
            to = jnp.where(direct[side], lax.rem(a + N_LAT - 1, N_LAT), a)
        return pltpu.make_async_remote_copy(
            src_ref=strip_to.at[p, side, pl.ds(source, count)],
            dst_ref=strip_from.at[p, 1 - side, first : first + count],
            send_sem=strip_send.at[p, side, part],
            recv_sem=strip_recv.at[p, 1 - side, part],
            device_id=(to, sides[side][1]),
            device_id_type=MESH,
        )

    for p in range(PAIRS):
        for i in (1, 2):
            load(i, p).wait()
        pack(p, 3, 7)

    answers = ((core == 0) & jnp.logical_not(is_first)) | is_last
    pl.semaphore_wait(barrier, N_NEAR + 2 * z + jnp.where(is_last, 3, jnp.where(answers, 1, 0)))

    def lat_copy(p, i, side):
        src = (k_hbm, v_hbm)[i]
        first_row = (0, ROWS - RADIUS)[side]
        return pltpu.make_async_remote_copy(
            src_ref=src.at[
                first_row : first_row + RADIUS, :, pl.ds(pl.multiple_of(p * LANES, LANES), LANES)
            ],
            dst_ref=(bot, top)[side].at[p, i],
            send_sem=lat_send.at[p, i, side],
            recv_sem=lat_recv.at[p, i, side],
            device_id=(up, down)[side],
            device_id_type=MESH,
        )

    def send_rows(p):
        for i in range(2):
            for side in range(2):
                lat_copy(p, i, side).start()

    def send_corners(side, first, last):
        for p in range(first, last):
            for part in (1, 2):
                strip_copy(p, side, part).start()

    sure = ((core == 1) | jnp.logical_not(is_first), (core == 0) | is_last)

    @pl.when(is_last)
    def _():
        send_corners(1, 0, CORNERS_FIRST)

    send_rows(0)
    for side in range(2):
        @pl.when(sure[side])
        def _():
            for p in range(PAIRS):
                strip_copy(p, side, 0).start()

    @pl.when(is_last)
    def _():
        send_corners(1, CORNERS_FIRST, PAIRS)

    for p in range(1, PAIRS):
        send_rows(p)

    @pl.when((core == 0) & jnp.logical_not(is_first))
    def _():
        pl.semaphore_signal(entered, inc=1, device_id=left, device_id_type=MESH)

    @pl.when(is_last)
    def _():
        for da in (-1, 0, 1):
            pl.semaphore_signal(entered, inc=1, device_id=diagonal(1, da), device_id_type=MESH)

    for d in range(1, N_Z):
        @pl.when(z - d >= 0)
        def _():
            for dh in range(2):
                pl.semaphore_signal(met, inc=1, device_id=across(-d, dh), device_id_type=MESH)

    key = lax.broadcasted_iota(jnp.int32, (EXT_ROWS * SPAN, QN), 0)
    query = lax.broadcasted_iota(jnp.int32, (EXT_ROWS * SPAN, QN), 1)
    key_row = key // SPAN - RADIUS
    row_gap = key_row - query // TILE
    col_gap = lax.rem(key, SPAN) - WIDE - lax.rem(query, TILE)
    whole_row = a * ROWS + key_row
    meets = (
        (row_gap >= -RADIUS) & (row_gap <= RADIUS) & (col_gap >= -RADIUS) & (col_gap <= RADIUS)
        & (whole_row >= 0) & (whole_row < N_LAT * ROWS)
    )
    mask[...] = jnp.where(meets, 1.0, 0.0)

    acc[...] = jnp.zeros_like(acc)
    sk[...] = jnp.zeros_like(sk)

    def stage_a(p):
        for i in range(2):
            for side in range(2):
                lat_copy(p, i, side).wait_recv()
        pack(p, 0, 3)
        pack(p, 7, 10)
        for side in range(2):
            @pl.when(jnp.logical_not(direct[side]))
            def _():
                for part in (1, 2):
                    strip_copy(p, side, part).start()

    def ext_middle(p):
        for r in range(EXT_ROWS):
            for i in range(2):
                ext[i, r, TILE : 2 * TILE] = rows_of(p, i, r)[WIDE : WIDE + TILE].astype(BF16)

    def ext_sides(p):
        for side in range(2):
            for part in range(3):
                strip_copy(p, side, part).wait_recv()
        for rp in range(EXT_ROWS // 2):
            for i in range(2):
                west = strip_from[p, 0, rp, i].astype(F32)
                east = strip_from[p, 1, rp, i].astype(F32)
                for j in range(2):
                    r = 2 * rp + j
                    half = slice(j * WIDE, (j + 1) * WIDE)
                    center = rows_of(p, i, r)
                    ext[i, r, :TILE] = jnp.concatenate([west[half], center[:WIDE]], 0).astype(BF16)
                    ext[i, r, 2 * TILE :] = jnp.concatenate(
                        [center[COLS - WIDE :], east[half]], 0
                    ).astype(BF16)

    def place(tile):
        at = tile * TILE
        return slice(at, at + TILE), slice(at, at + SPAN)

    def lanes(p):
        return pl.ds(pl.multiple_of(p * LANES, LANES), LANES)

    def turned(ref, p, cols):
        return head_blocks(ref[p, :, cols, :].reshape(QN, LANES).astype(F32).T)

    def forward(p, tile):
        cols, span = place(tile)
        q_low = (turned(q_s, p, cols) * (1.0 / 64.0)).astype(BF16)
        lane = lax.broadcasted_iota(jnp.int32, (1, 2 * QN), 1)
        sink = jnp.exp(jnp.where(lane < QN, sink_ref[2 * p], sink_ref[2 * p + 1]))
        k_here = ext[0, :, span, :].reshape(KEYS, LANES)
        v_here = ext[1, :, span, :].reshape(KEYS, LANES)
        g_blocks = turned(g_s, p, cols)
        squashed = jnp.tanh(dot(k_here, q_low))
        meets_here = mask[...]
        weight = jnp.exp2(squashed * EXP2_RATE) * jnp.concatenate([meets_here, meets_here], 1)
        total = jnp.sum(weight.reshape(KEYS // 8, 8, 2 * QN), axis=0)
        weight_low = weight.astype(BF16)
        e_s[tile] = weight_low
        u_s[tile] = (weight * (1.0 - squashed * squashed)).astype(BF16)
        prob_s[tile] = dot(v_here, g_blocks.astype(BF16))
        out = dot(v_here, weight_low, TN)
        inverse = 1.0 / (jnp.sum(total, axis=0, keepdims=True) + sink)
        out = out * inverse
        delta = jnp.sum(g_blocks * out, axis=0, keepdims=True)
        rate[tile, 0] = jnp.broadcast_to(inverse, (8, 2 * QN))
        rate[tile, 1] = jnp.broadcast_to(delta, (8, 2 * QN))
        o_ref[:, cols, lanes(p)] = own_heads(out).T.reshape(ROWS, TILE, LANES).astype(BF16)
        share = sink * inverse * delta
        sk[p, :, :] = sk[p, :, :] - jnp.concatenate([share[:, :QN], share[:, QN:]], 0)

    def backward(p, tile):
        cols, span = place(tile)
        inverse = rate[tile, 0, 0:1, :]
        delta = rate[tile, 1, 0:1, :]
        g_blocks = turned(g_s, p, cols)
        q_back = (turned(q_s, p, cols) * (inverse * 0.125)).astype(BF16)
        g_back = (g_blocks * inverse).astype(BF16)
        k_here = ext[0, :, span, :].reshape(KEYS, LANES)
        score = (u_s[tile].astype(F32) * (prob_s[tile] - delta)).astype(BF16)
        dk = dot(score, q_back, NT)
        dv = dot(e_s[tile], g_back, NT)
        dq = dot(k_here, score, TN)
        acc[p, 0, :, span, :] += dk.reshape(EXT_ROWS, SPAN, LANES)
        acc[p, 1, :, span, :] += dv.reshape(EXT_ROWS, SPAN, LANES)
        dq = dq * (inverse * 0.125)
        dq_ref[:, cols, lanes(p)] = own_heads(dq).T.reshape(ROWS, TILE, LANES).astype(BF16)

    def gs_copy(p, side, part):
        first, count = spans[part]
        to, lands = a, first
        if part == 1:
            to = jnp.where(direct[side], lax.rem(a + N_LAT - 1, N_LAT), a)
            lands = jnp.where(direct[side], 7, 0)
        if part == 2:
            to = jnp.where(direct[side], lax.rem(a + 1, N_LAT), a)
            lands = jnp.where(direct[side], 0, 7)
        sem = part if part == 0 else jnp.where(direct[side], 3 - part, part)
        return pltpu.make_async_remote_copy(
            src_ref=gstrip_to.at[p, side, first : first + count],
            dst_ref=gstrip_from.at[p, 1 - side, pl.ds(lands, count)],
            send_sem=gs_send.at[p, side, sem],
            recv_sem=gs_recv.at[p, 1 - side, sem],
            device_id=(to, sides[side][1]),
            device_id_type=MESH,
        )

    def send_strips(p, side):
        first = side * (COLS + WIDE)
        for rp in range(EXT_ROWS // 2):
            for i in range(2):
                both = acc[p, i, 2 * rp : 2 * rp + 2, first : first + WIDE, :]
                gstrip_to[p, side, rp, i] = both.reshape(2 * WIDE, LANES).astype(BF16)

    def start_strips(p):
        for side in range(2):
            for part in (1, 2, 0):
                gs_copy(p, side, part).start()

    def rim_copy(p, side):
        return pltpu.make_async_remote_copy(
            src_ref=rim_to.at[p, side],
            dst_ref=rim_from.at[p, 1 - side],
            send_sem=rim_send.at[p, side],
            recv_sem=rim_recv.at[p, 1 - side],
            device_id=(up, down)[side],
            device_id_type=MESH,
        )

    def add_strip(p, side, rp, row):
        first = (WIDE, COLS)[side]
        for i in range(2):
            came = gstrip_from[p, side, rp, i].astype(F32).reshape(2, WIDE, LANES)
            acc[p, i, pl.ds(row, 2), first : first + WIDE, :] += came

    def stage_c(p):
        for side in range(2):
            @pl.when(jnp.logical_not(direct[side]))
            def _():
                for part in (1, 2):
                    gs_copy(p, 1 - side, part).wait_recv()
                for rp in (0, 1, 2, 7, 8, 9):
                    add_strip(p, side, rp, 2 * rp)
        for i in range(2):
            for r in range(RADIUS):
                rim_to[p, 0, i, r] = acc[p, i, r, WIDE : WIDE + COLS, :].astype(BF16)
                rim_to[p, 1, i, r] = acc[p, i, RADIUS + ROWS + r, WIDE : WIDE + COLS, :].astype(BF16)
        for side in range(2):
            rim_copy(p, side).start()

    def stage_d(p):
        for side in range(2):
            gs_copy(p, 1 - side, 0).wait_recv()
            for rp in (3, 4, 5, 6):
                add_strip(p, side, rp, 2 * rp)

            @pl.when(direct[side])
            def _():
                for part in (1, 2):
                    gs_copy(p, 1 - side, part).wait_recv()
                for rp in range(3):
                    add_strip(p, side, rp, 2 * rp + RADIUS)
                    add_strip(p, side, rp + 7, 2 * rp + RADIUS + 2)
        for side in range(2):
            rim_copy(p, side).wait_recv()
        for i in range(2):
            for r in range(ROWS):
                total = acc[p, i, RADIUS + r, WIDE : WIDE + COLS, :]
                if r < RADIUS:
                    total = total + rim_from[p, 0, i, r].astype(F32)
                if r >= ROWS - RADIUS:
                    total = total + rim_from[p, 1, i, r - (ROWS - RADIUS)].astype(F32)
                (dk_ref, dv_ref)[i][r, :, lanes(p)] = total.astype(BF16)

    def skp_copy(d):
        return pltpu.make_async_remote_copy(
            src_ref=sk_plane.at[0], dst_ref=sk_plane.at[d],
            send_sem=skp_send.at[d], recv_sem=skp_recv.at[d],
            device_id=near_peer(d), device_id_type=MESH,
        )

    def skz_copy(d):
        return pltpu.make_async_remote_copy(
            src_ref=sk_z.at[0], dst_ref=sk_z.at[d],
            send_sem=skz_send.at[d], recv_sem=skz_recv.at[d],
            device_id=far_peer(d), device_id_type=MESH,
        )

    sink_copy.wait()

    @pl.when((core == 1) & jnp.logical_not(is_last))
    def _():
        pl.semaphore_wait(entered, 1)
        for p in range(PAIRS):
            strip_copy(p, 1, 0).start()

    stage_a(0)
    stage_a(1)

    @pl.when(is_first)
    def _():
        pl.semaphore_wait(entered, 3)
        for p in range(PAIRS):
            for part in (1, 2, 0):
                strip_copy(p, 0, part).start()
        stage_a(2)
        stage_a(3)

    def gather(p):
        for i in (0, 3):
            load(i, p).wait()
        ext_middle(p)
        ext_sides(p)

    def forward_both(p):
        forward(p, 0)
        forward(p, 1)

    def backward_both(p):
        backward(p, 0)
        backward(p, 1)
        send_strips(p, 0)
        send_strips(p, 1)
        start_strips(p)

    def step(p, carry):
        gather(p)
        forward_both(p)
        backward_both(p)

        @pl.when((p < PAIRS - 2) & jnp.logical_not(is_first))
        def _():
            stage_a(p + 2)

        @pl.when(p > 0)
        def _():
            stage_c(p - 1)

        return carry

    lax.fori_loop(0, PAIRS - 1, step, 0)
    gather(PAIRS - 1)
    forward_both(PAIRS - 1)
    heads = jnp.sum(sk[...].reshape(2 * PAIRS, QN), axis=1, keepdims=True)
    row = lax.broadcasted_iota(jnp.int32, (2 * PAIRS, QN), 0)
    column_of = lax.broadcasted_iota(jnp.int32, (2 * PAIRS, QN), 1)
    sk_plane[0] = jnp.sum(jnp.where(row == column_of, heads, 0.0), axis=0, keepdims=True)
    for d in range(1, N_NEAR):
        skp_copy(d).start()
    backward_both(PAIRS - 1)
    stage_c(PAIRS - 2)
    for d in range(1, N_NEAR):
        skp_copy(d).wait_recv()
    sk_z[0] = jnp.sum(sk_plane[...], axis=0)

    @pl.when(z < N_Z - 1)
    def _():
        pl.semaphore_wait(met, 2 * (N_Z - 1 - z))

    for d in range(1, N_FAR):
        skz_copy(d).start()

    stage_c(PAIRS - 1)

    def finish(p, carry):
        stage_d(p)
        return carry

    lax.fori_loop(0, PAIRS, finish, 0)
    for d in range(1, N_FAR):
        skz_copy(d).wait_recv()
    sg_ref[...] = jnp.sum(sk_z[...], axis=0)

    for p in range(PAIRS):
        for side in range(2):
            for i in range(2):
                lat_copy(p, i, side).wait_send()
            for part in range(3):
                strip_copy(p, side, part).wait_send()
                gs_copy(p, side, part).wait_send()
            rim_copy(p, side).wait_send()
    for d in range(1, N_NEAR):
        skp_copy(d).wait_send()
    for d in range(1, N_FAR):
        skz_copy(d).wait_send()


def place_results(o_ref, dq_ref, dk_ref, dv_ref, sg_ref, o_out, dq_out, dk_out, dv_out, sg_out, sem):
    sources = (o_ref, dq_ref, dk_ref, dv_ref)
    stores = [
        pltpu.make_async_copy(sources[i], there, sem.at[i])
        for i, there in enumerate((o_out, dq_out, dk_out, dv_out))
    ]
    for store in stores:
        store.start()
    sg_out[...] = sg_ref[0, : 2 * PAIRS]
    for store in stores:
        store.wait()


def on_device(queries, keys, values, grad_out, sink_logits):
    shape = jax.ShapeDtypeStruct(queries.shape, BF16)
    anywhere = pl.BlockSpec(memory_space=pl.ANY)
    dma = pltpu.SemaphoreType.DMA
    vmem = pl.BlockSpec(memory_space=pltpu.VMEM)
    results = pl.pallas_call(
        kernel,
        out_shape=(pltpu.VMEM(queries.shape, BF16),) * 4 + (pltpu.VMEM((1, QN), F32),),
        in_specs=[anywhere] * 5,
        out_specs=(vmem,) * 5,
        scratch_shapes=[
            pltpu.SMEM((2 * PAIRS,), F32),
            pltpu.VMEM((PAIRS, ROWS, COLS, LANES), BF16),
            pltpu.VMEM((2, PAIRS, ROWS, COLS, LANES), BF16),
            pltpu.VMEM((PAIRS, ROWS, COLS, LANES), BF16),
            pltpu.VMEM((2, EXT_ROWS, EXT_COLS, LANES), BF16),
            pltpu.VMEM((PAIRS, 2, RADIUS, COLS, LANES), BF16),
            pltpu.VMEM((PAIRS, 2, RADIUS, COLS, LANES), BF16),
            pltpu.VMEM((EXT_ROWS * SPAN, QN), F32),
            pltpu.VMEM((PAIRS, 2, EXT_ROWS // 2, 2, 2 * WIDE, LANES), BF16),
            pltpu.VMEM((PAIRS, 2, EXT_ROWS // 2, 2, 2 * WIDE, LANES), BF16),
            pltpu.VMEM((PAIRS, 2, EXT_ROWS // 2, 2, 2 * WIDE, LANES), BF16),
            pltpu.VMEM((PAIRS, 2, EXT_ROWS // 2, 2, 2 * WIDE, LANES), BF16),
            pltpu.VMEM((PAIRS, 2, 2, RADIUS, COLS, LANES), BF16),
            pltpu.VMEM((PAIRS, 2, 2, RADIUS, COLS, LANES), BF16),
            pltpu.VMEM((PAIRS, 2, EXT_ROWS, EXT_COLS, LANES), F32),
            pltpu.VMEM((2, EXT_ROWS * SPAN, 2 * QN), BF16),
            pltpu.VMEM((2, EXT_ROWS * SPAN, 2 * QN), BF16),
            pltpu.VMEM((2, EXT_ROWS * SPAN, 2 * QN), F32),
            pltpu.VMEM((2, 2, 8, 2 * QN), F32),
            pltpu.VMEM((PAIRS, 2, QN), F32),
            pltpu.VMEM((N_NEAR, 1, QN), F32),
            pltpu.VMEM((N_FAR, 1, QN), F32),
            dma(()),
            dma((4, PAIRS)),
            dma((PAIRS, 2, 2)),
            dma((PAIRS, 2, 2)),
            dma((PAIRS, 2, 3)),
            dma((PAIRS, 2, 3)),
            dma((PAIRS, 2, 3)),
            dma((PAIRS, 2, 3)),
            dma((PAIRS, 2)),
            dma((PAIRS, 2)),
            dma((N_NEAR,)),
            dma((N_NEAR,)),
            dma((N_FAR,)),
            dma((N_FAR,)),
            pltpu.SemaphoreType.REGULAR,
            pltpu.SemaphoreType.REGULAR,
        ],
        compiler_params=pltpu.CompilerParams(
            collective_id=0, has_side_effects=True, vmem_limit_bytes=60 * 1024 * 1024
        ),
    )(queries, keys, values, grad_out, sink_logits)
    results = [pltpu.with_memory_space_constraint(result, pltpu.VMEM) for result in results]
    return pl.pallas_call(
        place_results,
        out_shape=(shape,) * 4 + (jax.ShapeDtypeStruct((2 * PAIRS,), F32),),
        in_specs=[anywhere] * 4 + [vmem],
        out_specs=(anywhere,) * 4 + (vmem,),
        scratch_shapes=[dma((4,))],
    )(*results)


def solution(mesh):
    cells = P("lat", "lon", None)
    return jax.shard_map(
        on_device,
        mesh=mesh,
        in_specs=(cells,) * 4 + (P(),),
        out_specs=(cells,) * 4 + (P(),),
        check_vma=False,
    )
```

```python
import functools
import math

import jax
import jax.numpy as jnp
from jax import lax
from jax.experimental import pallas as pl
from jax.experimental.pallas import tpu as pltpu
from jax.sharding import PartitionSpec as P

WIN = 13
RADIUS = WIN // 2
SOFTCAP = 8.0
PAIRS = 4
ROWS = 8
COLS = 32
WIDE = 8
CORNERS_FIRST = 2
EXT_ROWS = ROWS + 2 * RADIUS
EXT_COLS = COLS + 2 * WIDE
TILE = 16
SPAN = TILE + 2 * WIDE
KEYS = EXT_ROWS * SPAN
QN = ROWS * TILE
LANES = 128
N_LAT = 8
N_LON = 32
N_Z = 8
N_NEAR = 2 * N_LAT
N_FAR = 2 * N_Z
MESH = pl.DeviceIdType.MESH
BF16 = jnp.bfloat16
F32 = jnp.float32
EXP2_RATE = SOFTCAP * math.log2(math.e)

NT = (((1,), (1,)), ((), ()))
TN = (((0,), (0,)), ((), ()))


def dot(a, b, dims=(((1,), (0,)), ((), ()))):
    return lax.dot_general(a, b, dims, preferred_element_type=F32)


def head_blocks(turned):
    first = lax.broadcasted_iota(jnp.int32, (LANES, QN), 0) < LANES // 2
    return jnp.concatenate(
        [jnp.where(first, turned, 0.0), jnp.where(first, 0.0, turned)], axis=1
    )


def own_heads(both):
    first = lax.broadcasted_iota(jnp.int32, (LANES, QN), 0) < LANES // 2
    return jnp.where(first, both[:, :QN], both[:, QN:])


def kernel(
    q_hbm, k_hbm, v_hbm, g_hbm, sink_hbm,
    o_ref, dq_ref, dk_ref, dv_ref, sg_ref,
    sink_ref, q_s, kv_s, g_s, ext, top, bot, mask,
    strip_to, strip_from, gstrip_to, gstrip_from, rim_to, rim_from,
    acc, e_s, u_s, prob_s, rate, sk, sk_plane, sk_z,
    sink_sem, in_sem, lat_send, lat_recv, strip_send, strip_recv,
    gs_send, gs_recv, rim_send, rim_recv, skp_send, skp_recv, skz_send, skz_recv, entered, met,
):
    a = lax.axis_index("lat")
    b = lax.axis_index("lon")
    up = (lax.rem(a + N_LAT - 1, N_LAT), b)
    down = (lax.rem(a + 1, N_LAT), b)
    left = (a, lax.rem(b + N_LON - 1, N_LON))
    right = (a, lax.rem(b + 1, N_LON))
    sides = (left, right)
    column = lax.rem(b, 2 * N_Z)
    z = column // 2
    is_first = column == 0
    is_last = column == 2 * N_Z - 1

    core = lax.rem(b, 2)
    crossing = (left[1], right[1])

    def diagonal(side, da):
        return (lax.rem(a + da + N_LAT, N_LAT), crossing[side])

    half = b // (2 * N_Z)

    def near_peer(d):
        other = lax.rem(2 * a + core + d, N_NEAR)
        return (other // 2, lax.rem(other, 2) + 2 * z + 2 * N_Z * half)

    def across(dz, dh):
        return (a, core + 2 * lax.rem(z + dz + N_Z, N_Z) + 2 * N_Z * lax.rem(half + dh, 2))

    def far_peer(d):
        other = lax.rem(2 * z + half + d, N_FAR)
        return (a, core + 2 * (other // 2) + 2 * N_Z * lax.rem(other, 2))

    def load(i, p):
        src = (q_hbm, k_hbm, v_hbm, g_hbm)[i]
        dst = (q_s, kv_s.at[0], kv_s.at[1], g_s)[i]
        return pltpu.make_async_copy(
            src.at[:, :, pl.ds(pl.multiple_of(p * LANES, LANES), LANES)], dst.at[p], in_sem.at[i, p]
        )

    for p in range(PAIRS):
        for i in (1, 2):
            load(i, p).start()
    for p in range(PAIRS):
        for i in (0, 3):
            load(i, p).start()

    sink_copy = pltpu.make_async_copy(sink_hbm, sink_ref, sink_sem)
    sink_copy.start()
    barrier = pltpu.get_barrier_semaphore()

    def greet(device):
        pl.semaphore_signal(barrier, inc=1, device_id=device, device_id_type=MESH)

    for d in range(1, N_NEAR):
        greet(near_peer(d))
    greet(across(0, 1))

    @pl.when((core == 1) & jnp.logical_not(is_last))
    def _():
        greet(right)

    @pl.when(is_first)
    def _():
        for da in (-1, 0, 1):
            greet(diagonal(0, da))

    for d in range(1, N_Z):
        @pl.when(z + d < N_Z)
        def _():
            greet(across(d, 0))
            greet(across(d, 1))

    def rows_of(p, i, r):
        if r < RADIUS:
            return top[p, i, r].astype(F32)
        if r < RADIUS + ROWS:
            return kv_s[i, p, r - RADIUS].astype(F32)
        return bot[p, i, r - RADIUS - ROWS].astype(F32)

    def pack(p, first, last):
        for rp in range(first, last):
            for i in range(2):
                upper, lower = rows_of(p, i, 2 * rp), rows_of(p, i, 2 * rp + 1)
                strip_to[p, 0, rp, i] = jnp.concatenate([upper[:WIDE], lower[:WIDE]], 0).astype(BF16)
                strip_to[p, 1, rp, i] = jnp.concatenate(
                    [upper[COLS - WIDE :], lower[COLS - WIDE :]], 0
                ).astype(BF16)

    spans = ((3, 4), (0, 3), (7, 3))

    direct = (is_first, is_last)

    def strip_copy(p, side, part):
        first, count = spans[part]
        source, to = first, a
        if part == 1:
            source, to = jnp.where(direct[side], 4, 0), jnp.where(direct[side], lax.rem(a + 1, N_LAT), a)
        if part == 2:
            source = jnp.where(direct[side], 3, 7)
            to = jnp.where(direct[side], lax.rem(a + N_LAT - 1, N_LAT), a)
        return pltpu.make_async_remote_copy(
            src_ref=strip_to.at[p, side, pl.ds(source, count)],
            dst_ref=strip_from.at[p, 1 - side, first : first + count],
            send_sem=strip_send.at[p, side, part],
            recv_sem=strip_recv.at[p, 1 - side, part],
            device_id=(to, sides[side][1]),
            device_id_type=MESH,
        )

    for p in range(PAIRS):
        for i in (1, 2):
            load(i, p).wait()
        pack(p, 3, 7)

    answers = ((core == 0) & jnp.logical_not(is_first)) | is_last
    pl.semaphore_wait(barrier, N_NEAR + 2 * z + jnp.where(is_last, 3, jnp.where(answers, 1, 0)))

    goes = (a > 0, a < N_LAT - 1)

    @pl.when(a == 0)
    def _():
        top[...] = jnp.zeros_like(top)
        rim_from[:, 0] = jnp.zeros((PAIRS, 2, RADIUS, COLS, LANES), BF16)

    @pl.when(a == N_LAT - 1)
    def _():
        bot[...] = jnp.zeros_like(bot)
        rim_from[:, 1] = jnp.zeros((PAIRS, 2, RADIUS, COLS, LANES), BF16)

    def lat_copy(p, i, side):
        src = (k_hbm, v_hbm)[i]
        first_row = (0, ROWS - RADIUS)[side]
        return pltpu.make_async_remote_copy(
            src_ref=src.at[
                first_row : first_row + RADIUS, :, pl.ds(pl.multiple_of(p * LANES, LANES), LANES)
            ],
            dst_ref=(bot, top)[side].at[p, i],
            send_sem=lat_send.at[p, i, side],
            recv_sem=lat_recv.at[p, i, side],
            device_id=(up, down)[side],
            device_id_type=MESH,
        )

    def send_rows(p):
        for side in range(2):
            @pl.when(goes[side])
            def _():
                for i in range(2):
                    lat_copy(p, i, side).start()

    def send_corners(side, first, last):
        for p in range(first, last):
            for part in (1, 2):
                strip_copy(p, side, part).start()

    sure = ((core == 1) | jnp.logical_not(is_first), (core == 0) | is_last)

    @pl.when(is_last)
    def _():
        send_corners(1, 0, CORNERS_FIRST)

    send_rows(0)
    for side in range(2):
        @pl.when(sure[side])
        def _():
            for p in range(PAIRS):
                strip_copy(p, side, 0).start()

    @pl.when(is_last)
    def _():
        send_corners(1, CORNERS_FIRST, PAIRS)

    for p in range(1, PAIRS):
        send_rows(p)

    @pl.when((core == 0) & jnp.logical_not(is_first))
    def _():
        pl.semaphore_signal(entered, inc=1, device_id=left, device_id_type=MESH)

    @pl.when(is_last)
    def _():
        for da in (-1, 0, 1):
            pl.semaphore_signal(entered, inc=1, device_id=diagonal(1, da), device_id_type=MESH)

    for d in range(1, N_Z):
        @pl.when(z - d >= 0)
        def _():
            for dh in range(2):
                pl.semaphore_signal(met, inc=1, device_id=across(-d, dh), device_id_type=MESH)

    key = lax.broadcasted_iota(jnp.int32, (EXT_ROWS * SPAN, QN), 0)
    query = lax.broadcasted_iota(jnp.int32, (EXT_ROWS * SPAN, QN), 1)
    key_row = key // SPAN - RADIUS
    row_gap = key_row - query // TILE
    col_gap = lax.rem(key, SPAN) - WIDE - lax.rem(query, TILE)
    whole_row = a * ROWS + key_row
    meets = (
        (row_gap >= -RADIUS) & (row_gap <= RADIUS) & (col_gap >= -RADIUS) & (col_gap <= RADIUS)
        & (whole_row >= 0) & (whole_row < N_LAT * ROWS)
    )
    mask[...] = jnp.where(meets, 1.0, 0.0)

    acc[...] = jnp.zeros_like(acc)
    sk[...] = jnp.zeros_like(sk)

    def stage_a(p):
        for side in range(2):
            @pl.when(goes[1 - side])
            def _():
                for i in range(2):
                    lat_copy(p, i, side).wait_recv()
        pack(p, 0, 3)
        pack(p, 7, 10)
        for side in range(2):
            @pl.when(jnp.logical_not(direct[side]))
            def _():
                for part in (1, 2):
                    strip_copy(p, side, part).start()

    def ext_middle(p):
        for r in range(EXT_ROWS):
            for i in range(2):
                ext[i, r, TILE : 2 * TILE] = rows_of(p, i, r)[WIDE : WIDE + TILE].astype(BF16)

    def ext_sides(p):
        for side in range(2):
            for part in range(3):
                strip_copy(p, side, part).wait_recv()
        for rp in range(EXT_ROWS // 2):
            for i in range(2):
                west = strip_from[p, 0, rp, i].astype(F32)
                east = strip_from[p, 1, rp, i].astype(F32)
                for j in range(2):
                    r = 2 * rp + j
                    half = slice(j * WIDE, (j + 1) * WIDE)
                    center = rows_of(p, i, r)
                    ext[i, r, :TILE] = jnp.concatenate([west[half], center[:WIDE]], 0).astype(BF16)
                    ext[i, r, 2 * TILE :] = jnp.concatenate(
                        [center[COLS - WIDE :], east[half]], 0
                    ).astype(BF16)

    def place(tile):
        at = tile * TILE
        return slice(at, at + TILE), slice(at, at + SPAN)

    def lanes(p):
        return pl.ds(pl.multiple_of(p * LANES, LANES), LANES)

    def turned(ref, p, cols):
        return head_blocks(ref[p, :, cols, :].reshape(QN, LANES).astype(F32).T)

    def forward(p, tile):
        cols, span = place(tile)
        q_low = (turned(q_s, p, cols) * (1.0 / 64.0)).astype(BF16)
        lane = lax.broadcasted_iota(jnp.int32, (1, 2 * QN), 1)
        sink = jnp.exp(jnp.where(lane < QN, sink_ref[2 * p], sink_ref[2 * p + 1]))
        k_here = ext[0, :, span, :].reshape(KEYS, LANES)
        v_here = ext[1, :, span, :].reshape(KEYS, LANES)
        g_blocks = turned(g_s, p, cols)
        squashed = jnp.tanh(dot(k_here, q_low))
        meets_here = mask[...]
        weight = jnp.exp2(squashed * EXP2_RATE) * jnp.concatenate([meets_here, meets_here], 1)
        total = jnp.sum(weight.reshape(KEYS // 8, 8, 2 * QN), axis=0)
        weight_low = weight.astype(BF16)
        e_s[tile] = weight_low
        u_s[tile] = (weight * (1.0 - squashed * squashed)).astype(BF16)
        prob_s[tile] = dot(v_here, g_blocks.astype(BF16))
        out = dot(v_here, weight_low, TN)
        inverse = 1.0 / (jnp.sum(total, axis=0, keepdims=True) + sink)
        out = out * inverse
        delta = jnp.sum(g_blocks * out, axis=0, keepdims=True)
        rate[tile, 0] = jnp.broadcast_to(inverse, (8, 2 * QN))
        rate[tile, 1] = jnp.broadcast_to(delta, (8, 2 * QN))
        o_ref[:, cols, lanes(p)] = own_heads(out).T.reshape(ROWS, TILE, LANES).astype(BF16)
        share = sink * inverse * delta
        sk[p, :, :] = sk[p, :, :] - jnp.concatenate([share[:, :QN], share[:, QN:]], 0)

    def backward(p, tile):
        cols, span = place(tile)
        inverse = rate[tile, 0, 0:1, :]
        delta = rate[tile, 1, 0:1, :]
        g_blocks = turned(g_s, p, cols)
        q_back = (turned(q_s, p, cols) * (inverse * 0.125)).astype(BF16)
        g_back = (g_blocks * inverse).astype(BF16)
        k_here = ext[0, :, span, :].reshape(KEYS, LANES)
        score = (u_s[tile].astype(F32) * (prob_s[tile] - delta)).astype(BF16)
        dk = dot(score, q_back, NT)
        dv = dot(e_s[tile], g_back, NT)
        dq = dot(k_here, score, TN)
        acc[p, 0, :, span, :] += dk.reshape(EXT_ROWS, SPAN, LANES)
        acc[p, 1, :, span, :] += dv.reshape(EXT_ROWS, SPAN, LANES)
        dq = dq * (inverse * 0.125)
        dq_ref[:, cols, lanes(p)] = own_heads(dq).T.reshape(ROWS, TILE, LANES).astype(BF16)

    def gs_copy(p, side, part):
        first, count = spans[part]
        to, lands = a, first
        if part == 1:
            to = jnp.where(direct[side], lax.rem(a + N_LAT - 1, N_LAT), a)
            lands = jnp.where(direct[side], 7, 0)
        if part == 2:
            to = jnp.where(direct[side], lax.rem(a + 1, N_LAT), a)
            lands = jnp.where(direct[side], 0, 7)
        sem = part if part == 0 else jnp.where(direct[side], 3 - part, part)
        return pltpu.make_async_remote_copy(
            src_ref=gstrip_to.at[p, side, first : first + count],
            dst_ref=gstrip_from.at[p, 1 - side, pl.ds(lands, count)],
            send_sem=gs_send.at[p, side, sem],
            recv_sem=gs_recv.at[p, 1 - side, sem],
            device_id=(to, sides[side][1]),
            device_id_type=MESH,
        )

    def send_strips(p, side):
        first = side * (COLS + WIDE)
        for rp in range(EXT_ROWS // 2):
            for i in range(2):
                both = acc[p, i, 2 * rp : 2 * rp + 2, first : first + WIDE, :]
                gstrip_to[p, side, rp, i] = both.reshape(2 * WIDE, LANES).astype(BF16)

    def start_strips(p):
        for side in range(2):
            for part in (1, 2, 0):
                gs_copy(p, side, part).start()

    def rim_copy(p, side):
        return pltpu.make_async_remote_copy(
            src_ref=rim_to.at[p, side],
            dst_ref=rim_from.at[p, 1 - side],
            send_sem=rim_send.at[p, side],
            recv_sem=rim_recv.at[p, 1 - side],
            device_id=(up, down)[side],
            device_id_type=MESH,
        )

    def add_strip(p, side, rp, row):
        first = (WIDE, COLS)[side]
        for i in range(2):
            came = gstrip_from[p, side, rp, i].astype(F32).reshape(2, WIDE, LANES)
            acc[p, i, pl.ds(row, 2), first : first + WIDE, :] += came

    def stage_c(p):
        for side in range(2):
            @pl.when(jnp.logical_not(direct[side]))
            def _():
                for part in (1, 2):
                    gs_copy(p, 1 - side, part).wait_recv()
                for rp in (0, 1, 2, 7, 8, 9):
                    add_strip(p, side, rp, 2 * rp)
        for i in range(2):
            for r in range(RADIUS):
                rim_to[p, 0, i, r] = acc[p, i, r, WIDE : WIDE + COLS, :].astype(BF16)
                rim_to[p, 1, i, r] = acc[p, i, RADIUS + ROWS + r, WIDE : WIDE + COLS, :].astype(BF16)
        for side in range(2):
            @pl.when(goes[side])
            def _():
                rim_copy(p, side).start()

    def stage_d(p):
        for side in range(2):
            gs_copy(p, 1 - side, 0).wait_recv()
            for rp in (3, 4, 5, 6):
                add_strip(p, side, rp, 2 * rp)

            @pl.when(direct[side])
            def _():
                for part in (1, 2):
                    gs_copy(p, 1 - side, part).wait_recv()
                for rp in range(3):
                    add_strip(p, side, rp, 2 * rp + RADIUS)
                    add_strip(p, side, rp + 7, 2 * rp + RADIUS + 2)
        for side in range(2):
            @pl.when(goes[1 - side])
            def _():
                rim_copy(p, side).wait_recv()
        for i in range(2):
            for r in range(ROWS):
                total = acc[p, i, RADIUS + r, WIDE : WIDE + COLS, :]
                if r < RADIUS:
                    total = total + rim_from[p, 0, i, r].astype(F32)
                if r >= ROWS - RADIUS:
                    total = total + rim_from[p, 1, i, r - (ROWS - RADIUS)].astype(F32)
                (dk_ref, dv_ref)[i][r, :, lanes(p)] = total.astype(BF16)

    def skp_copy(d):
        return pltpu.make_async_remote_copy(
            src_ref=sk_plane.at[0], dst_ref=sk_plane.at[d],
            send_sem=skp_send.at[d], recv_sem=skp_recv.at[d],
            device_id=near_peer(d), device_id_type=MESH,
        )

    def skz_copy(d):
        return pltpu.make_async_remote_copy(
            src_ref=sk_z.at[0], dst_ref=sk_z.at[d],
            send_sem=skz_send.at[d], recv_sem=skz_recv.at[d],
            device_id=far_peer(d), device_id_type=MESH,
        )

    sink_copy.wait()

    @pl.when((core == 1) & jnp.logical_not(is_last))
    def _():
        pl.semaphore_wait(entered, 1)
        for p in range(PAIRS):
            strip_copy(p, 1, 0).start()

    stage_a(0)
    stage_a(1)

    @pl.when(is_first)
    def _():
        pl.semaphore_wait(entered, 3)
        for p in range(PAIRS):
            for part in (1, 2, 0):
                strip_copy(p, 0, part).start()
        stage_a(2)
        stage_a(3)

    def gather(p):
        for i in (0, 3):
            load(i, p).wait()
        ext_middle(p)
        ext_sides(p)

    def forward_both(p):
        forward(p, 0)
        forward(p, 1)

    def backward_both(p):
        backward(p, 0)
        backward(p, 1)
        send_strips(p, 0)
        send_strips(p, 1)
        start_strips(p)

    def step(p, carry):
        gather(p)
        forward_both(p)
        backward_both(p)

        @pl.when((p < PAIRS - 2) & jnp.logical_not(is_first))
        def _():
            stage_a(p + 2)

        @pl.when(p > 0)
        def _():
            stage_c(p - 1)

        return carry

    lax.fori_loop(0, PAIRS - 1, step, 0)
    gather(PAIRS - 1)
    forward_both(PAIRS - 1)
    heads = jnp.sum(sk[...].reshape(2 * PAIRS, QN), axis=1, keepdims=True)
    row = lax.broadcasted_iota(jnp.int32, (2 * PAIRS, QN), 0)
    column_of = lax.broadcasted_iota(jnp.int32, (2 * PAIRS, QN), 1)
    sk_plane[0] = jnp.sum(jnp.where(row == column_of, heads, 0.0), axis=0, keepdims=True)
    for d in range(1, N_NEAR):
        skp_copy(d).start()
    backward_both(PAIRS - 1)
    stage_c(PAIRS - 2)
    for d in range(1, N_NEAR):
        skp_copy(d).wait_recv()
    sk_z[0] = jnp.sum(sk_plane[...], axis=0)

    @pl.when(z < N_Z - 1)
    def _():
        pl.semaphore_wait(met, 2 * (N_Z - 1 - z))

    for d in range(1, N_FAR):
        skz_copy(d).start()

    stage_c(PAIRS - 1)

    def finish(p, carry):
        stage_d(p)
        return carry

    lax.fori_loop(0, PAIRS, finish, 0)
    for d in range(1, N_FAR):
        skz_copy(d).wait_recv()
    sg_ref[...] = jnp.sum(sk_z[...], axis=0)

    for p in range(PAIRS):
        for side in range(2):
            @pl.when(goes[side])
            def _():
                rim_copy(p, side).wait_send()
                for i in range(2):
                    lat_copy(p, i, side).wait_send()
            for part in range(3):
                strip_copy(p, side, part).wait_send()
                gs_copy(p, side, part).wait_send()
    for d in range(1, N_NEAR):
        skp_copy(d).wait_send()
    for d in range(1, N_FAR):
        skz_copy(d).wait_send()


def place_results(o_ref, dq_ref, dk_ref, dv_ref, sg_ref, o_out, dq_out, dk_out, dv_out, sg_out, sem):
    sources = (o_ref, dq_ref, dk_ref, dv_ref)
    stores = [
        pltpu.make_async_copy(sources[i], there, sem.at[i])
        for i, there in enumerate((o_out, dq_out, dk_out, dv_out))
    ]
    for store in stores:
        store.start()
    sg_out[...] = sg_ref[0, : 2 * PAIRS]
    for store in stores:
        store.wait()


def on_device(queries, keys, values, grad_out, sink_logits):
    shape = jax.ShapeDtypeStruct(queries.shape, BF16)
    anywhere = pl.BlockSpec(memory_space=pl.ANY)
    dma = pltpu.SemaphoreType.DMA
    vmem = pl.BlockSpec(memory_space=pltpu.VMEM)
    results = pl.pallas_call(
        kernel,
        out_shape=(pltpu.VMEM(queries.shape, BF16),) * 4 + (pltpu.VMEM((1, QN), F32),),
        in_specs=[anywhere] * 5,
        out_specs=(vmem,) * 5,
        scratch_shapes=[
            pltpu.SMEM((2 * PAIRS,), F32),
            pltpu.VMEM((PAIRS, ROWS, COLS, LANES), BF16),
            pltpu.VMEM((2, PAIRS, ROWS, COLS, LANES), BF16),
            pltpu.VMEM((PAIRS, ROWS, COLS, LANES), BF16),
            pltpu.VMEM((2, EXT_ROWS, EXT_COLS, LANES), BF16),
            pltpu.VMEM((PAIRS, 2, RADIUS, COLS, LANES), BF16),
            pltpu.VMEM((PAIRS, 2, RADIUS, COLS, LANES), BF16),
            pltpu.VMEM((EXT_ROWS * SPAN, QN), F32),
            pltpu.VMEM((PAIRS, 2, EXT_ROWS // 2, 2, 2 * WIDE, LANES), BF16),
            pltpu.VMEM((PAIRS, 2, EXT_ROWS // 2, 2, 2 * WIDE, LANES), BF16),
            pltpu.VMEM((PAIRS, 2, EXT_ROWS // 2, 2, 2 * WIDE, LANES), BF16),
            pltpu.VMEM((PAIRS, 2, EXT_ROWS // 2, 2, 2 * WIDE, LANES), BF16),
            pltpu.VMEM((PAIRS, 2, 2, RADIUS, COLS, LANES), BF16),
            pltpu.VMEM((PAIRS, 2, 2, RADIUS, COLS, LANES), BF16),
            pltpu.VMEM((PAIRS, 2, EXT_ROWS, EXT_COLS, LANES), F32),
            pltpu.VMEM((2, EXT_ROWS * SPAN, 2 * QN), BF16),
            pltpu.VMEM((2, EXT_ROWS * SPAN, 2 * QN), BF16),
            pltpu.VMEM((2, EXT_ROWS * SPAN, 2 * QN), F32),
            pltpu.VMEM((2, 2, 8, 2 * QN), F32),
            pltpu.VMEM((PAIRS, 2, QN), F32),
            pltpu.VMEM((N_NEAR, 1, QN), F32),
            pltpu.VMEM((N_FAR, 1, QN), F32),
            dma(()),
            dma((4, PAIRS)),
            dma((PAIRS, 2, 2)),
            dma((PAIRS, 2, 2)),
            dma((PAIRS, 2, 3)),
            dma((PAIRS, 2, 3)),
            dma((PAIRS, 2, 3)),
            dma((PAIRS, 2, 3)),
            dma((PAIRS, 2)),
            dma((PAIRS, 2)),
            dma((N_NEAR,)),
            dma((N_NEAR,)),
            dma((N_FAR,)),
            dma((N_FAR,)),
            pltpu.SemaphoreType.REGULAR,
            pltpu.SemaphoreType.REGULAR,
        ],
        compiler_params=pltpu.CompilerParams(
            collective_id=0, has_side_effects=True, vmem_limit_bytes=60 * 1024 * 1024
        ),
    )(queries, keys, values, grad_out, sink_logits)
    results = [pltpu.with_memory_space_constraint(result, pltpu.VMEM) for result in results]
    return pl.pallas_call(
        place_results,
        out_shape=(shape,) * 4 + (jax.ShapeDtypeStruct((2 * PAIRS,), F32),),
        in_specs=[anywhere] * 4 + [vmem],
        out_specs=(anywhere,) * 4 + (vmem,),
        scratch_shapes=[dma((4,))],
    )(*results)


def solution(mesh):
    cells = P("lat", "lon", None)
    return jax.shard_map(
        on_device,
        mesh=mesh,
        in_specs=(cells,) * 4 + (P(),),
        out_specs=(cells,) * 4 + (P(),),
        check_vma=False,
    )
```
